256 devices in a mesh: shot: 64 (over z, y, x_hi), slab: 4 (over x_lo, core).
Axes of the slice: x: 4 (x_hi: 2, x_lo: 2; x = x_hi * 2 + x_lo), y: 4, z: 8, core: 2. Of those that a mesh axis runs over, the one named last changes fastest.
Arguments:
- amplitudes: float32 [4, 6144], P('slab', 'shot'), may hold values from -6 to 6
- depth_cells: int32 [4, 6144], P('slab', 'shot'), may hold values from 0 to 63
- lateral_cells: int32 [2, 4, 6144], P(None, 'slab', 'shot'), may hold values from 0 to 511
- jitter: float32 [3, 4, 6144], P(None, 'slab', 'shot'), may hold values from 0 to 1
- tables: float32 [256, 4, 867], P('shot', 'slab'), may hold values from 2 to 509
- shot_cells: int32 [2, 256], P(None, 'shot'), may hold values from 0 to 511
- receiver_offsets: int32 [2, 256], replicated, may hold values from -64 to 63
- band_offsets: int32 [4], replicated, may hold values from 0 to 255
Outputs:
- synthetic: float32 [256, 256, 1024], P('shot')
- image: float32 [4, 6144], P('slab', 'shot')
The draws below stay inside these ranges and needn't reach their ends.
Inputs may be any that keep to these rules, and one draw needn't show every extreme that they name: Each slab's band lies inside the trace: band_offsets + 512 <= 1024.
All inputs are finite; a program needn't handle non-finite values.
Results may differ from the reference program's by a relative error of at most 0.009.
Values may be sent and summed in bfloat16 or wider, within the bound.
No kernel may reach another device: no remote copies, remote signals or barrier semaphores. Data moves between devices by JAX's collectives and lax.ppermute only.
A program may use at most 64 MiB of HBM per device.

```python
import math
import jax
import jax.numpy as jnp
from jax import lax

NX = 512
ZS = 64
NT = 1024
BAND = 512
R = 256
SPACING = 32
NL = 17
ND = 3
NODES = 867
SHOTS = 256
SC = 6144
N_SLAB = 4


def touch_ends(array, stream_key, least, largest):
    shape = array.shape
    spot = [jax.random.randint(jax.random.fold_in(stream_key, axis), (), 0, shape[axis]) for axis in range(len(shape))]
    array = array.at[tuple(spot)].set(least)
    longest = shape.index(max(shape))
    spot[longest] = (spot[longest] + 1) % shape[longest]
    return array.at[tuple(spot)].set(largest)


def levels(key, shape, cuts, smallest, largest):
    factor_of, own = 1.0, jax.random.fold_in(key, 6)
    for position, parts in cuts:
        draws = jnp.exp(jax.random.uniform(jax.random.fold_in(own, position), (parts,), jnp.float32, smallest / len(cuts), largest / len(cuts)))
        factor_of = factor_of * jnp.repeat(draws, shape[position] // parts).reshape([-1 if axis == position else 1 for axis in range(len(shape))])
    return factor_of


def centred(rng, shape, width, most, split=(), kind=jnp.bfloat16):
    loudness = levels(rng, shape, split, -0.22, 0.18) if split else 1.0
    entries = jax.random.normal(rng, shape, jnp.float32) * width * loudness
    return jnp.minimum(jnp.maximum(entries, -most), most).astype(kind)


def setup_inputs(seed: int = 0) -> dict:
    streams_of = jax.random.split(jax.random.key(seed), 9)
    amplitudes = centred(streams_of[0], (N_SLAB, SC), 1.0, 6.0, ((0, 4), (1, 64)), jnp.float32)
    depth_cells = touch_ends(jax.random.randint(streams_of[1], (N_SLAB, SC), 0, ZS), jax.random.fold_in(streams_of[1], 1), 0, ZS - 1).astype(jnp.int32)
    lateral_cells = touch_ends(jax.random.randint(streams_of[2], (2, N_SLAB, SC), 0, NX), jax.random.fold_in(streams_of[2], 1), 0, NX - 1).astype(jnp.int32)
    jitter = jnp.clip(1.0 * jax.random.uniform(streams_of[3], (3, N_SLAB, SC), jnp.float32) ** levels(streams_of[3], (3, N_SLAB, SC), ((1, 4), (2, 64)), -0.2, 0.2), 0.0, 1.0)
    tables = jnp.clip(2.0 + 507.0 * jax.random.uniform(streams_of[4], (SHOTS, N_SLAB, NODES), jnp.float32) ** levels(streams_of[4], (SHOTS, N_SLAB, NODES), ((0, 64), (1, 4)), -0.2, 0.2), 2.0, 509.0)
    shot_cells = touch_ends(jax.random.randint(streams_of[5], (2, SHOTS), 0, NX), jax.random.fold_in(streams_of[5], 1), 0, NX - 1).astype(jnp.int32)
    receiver_offsets = touch_ends(jax.random.randint(streams_of[6], (2, R), 0 - NX // 8, NX // 8), jax.random.fold_in(streams_of[6], 1), 0 - NX // 8, (NX // 8) - 1).astype(jnp.int32)
    band_offsets = touch_ends(jax.random.randint(streams_of[7], (N_SLAB,), 0, NT // 4), jax.random.fold_in(streams_of[7], 1), 0, (NT // 4) - 1).astype(jnp.int32)
    return {"amplitudes": amplitudes, "depth_cells": depth_cells, "lateral_cells": lateral_cells, "jitter": jitter, "tables": tables, "shot_cells": shot_cells, "receiver_offsets": receiver_offsets, "band_offsets": band_offsets}


def node_weights(coords):
    depth_nodes = jnp.arange(ND, dtype=jnp.float32)[:, None]
    lateral_nodes = jnp.arange(NL, dtype=jnp.float32)[:, None]
    weight_z = jnp.maximum(0.0, 1.0 - jnp.abs(coords[0][None, :] / SPACING - depth_nodes))
    weight_x = jnp.maximum(0.0, 1.0 - jnp.abs(coords[1][None, :] / SPACING - lateral_nodes))
    weight_y = jnp.maximum(0.0, 1.0 - jnp.abs(coords[2][None, :] / SPACING - lateral_nodes))
    joined = weight_z[:, None, None, :] * weight_x[None, :, None, :] * weight_y[None, None, :, :]
    return joined.reshape(ND * NL * NL, coords.shape[1])


def block_fields(coords, table, shot_xy, receivers):
    travel = jnp.dot(table, node_weights(coords), precision=lax.Precision.HIGHEST, preferred_element_type=jnp.float32)
    samples = jnp.arange(BAND, dtype=jnp.float32)
    hats = jnp.maximum(0.0, 1.0 - jnp.abs(samples[None, None, :] - travel[:, :, None])).astype(jnp.bfloat16)
    recv_x = shot_xy[0][:, None] + receivers[0][None, :]
    recv_y = shot_xy[1][:, None] + receivers[1][None, :]
    delta_x = recv_x[:, :, None] - coords[1][None, None, :]
    delta_y = recv_y[:, :, None] - coords[2][None, None, :]
    aperture = NX / 32.0
    gain = 1.0 / (1.0 + (delta_x * delta_x + delta_y * delta_y) / (aperture * aperture))
    return hats, gain


def reference(amplitudes, depth_cells, lateral_cells, jitter, tables, shot_cells, receiver_offsets, band_offsets):
    shot_xy = shot_cells.astype(jnp.float32)
    receivers = receiver_offsets.astype(jnp.float32)
    count = amplitudes.shape[1]
    shots = tables.shape[0]
    block = math.gcd(count, 256)
    nblocks = count // block
    all_coords = []
    partials = []
    for slab_index in range(N_SLAB):
        coords = jnp.stack([
            depth_cells[slab_index].astype(jnp.float32) + jitter[0, slab_index],
            lateral_cells[0, slab_index].astype(jnp.float32) + jitter[1, slab_index],
            lateral_cells[1, slab_index].astype(jnp.float32) + jitter[2, slab_index],
            amplitudes[slab_index]])
        all_coords.append(coords)
        table = tables[:, slab_index, :]

        def demig_step(index, total, coords=coords, table=table):
            piece = lax.dynamic_slice_in_dim(coords, index * block, block, 1)
            hats, gain = block_fields(piece, table, shot_xy, receivers)
            weighted = (gain * piece[3][None, None, :]).astype(jnp.bfloat16)
            weighted = lax.optimization_barrier(weighted).astype(jnp.float32)
            hats_wide = lax.optimization_barrier(hats).astype(jnp.float32)
            return total + jnp.einsum('srp,spt->srt', weighted, hats_wide)

        start = jnp.zeros((shots, R, BAND), jnp.float32)
        partial_value = lax.fori_loop(0, nblocks, demig_step, start)
        partials.append(partial_value.astype(jnp.bfloat16))
    trace = jnp.zeros((shots, R, NT), jnp.float32)
    zero = jnp.zeros((), jnp.int32)
    for slab_index in range(N_SLAB):
        offset = band_offsets[slab_index].astype(jnp.int32)
        current = lax.dynamic_slice(trace, (zero, zero, offset), (shots, R, BAND))
        trace = lax.dynamic_update_slice(trace, current + partials[slab_index].astype(jnp.float32), (zero, zero, offset))
    images = []
    for slab_index in range(N_SLAB):
        offset = band_offsets[slab_index].astype(jnp.int32)
        band = lax.dynamic_slice(trace, (zero, zero, offset), (shots, R, BAND)).astype(jnp.bfloat16)
        band_wide = lax.optimization_barrier(band).astype(jnp.float32)
        coords = all_coords[slab_index]
        table = tables[:, slab_index, :]

        def mig_block(index, coords=coords, table=table, band_wide=band_wide):
            piece = lax.dynamic_slice_in_dim(coords, index * block, block, 1)
            hats, gain = block_fields(piece, table, shot_xy, receivers)
            gain_low = lax.optimization_barrier(gain.astype(jnp.bfloat16)).astype(jnp.float32)
            product = jnp.einsum('srp,srt->spt', gain_low, band_wide)
            return jnp.sum(product * hats.astype(jnp.float32), axis=(0, 2))

        values = lax.map(mig_block, jnp.arange(nblocks, dtype=jnp.int32))
        images.append(values.reshape(count) / R)
    return trace, jnp.stack(images)
```

```python
import functools

import jax
import jax.numpy as jnp
from jax import lax
from jax.experimental import pallas as pl
from jax.experimental.pallas import tpu as pltpu
from jax.sharding import PartitionSpec as P

NX = 512
NT = 1024
BAND = 512
HALF = 256
SPACING = 32
NL = 17
ND = 3
SPAN = 768
LANES = 128
NODE_ROWS = 24
NODE_COLS = 32
ROWS = 8
CHUNK = ROWS * LANES
BF = jnp.bfloat16
F32 = jnp.float32


def split3(value):
    first = value.astype(BF)
    rest = value - first.astype(F32)
    second = rest.astype(BF)
    third = (rest - second.astype(F32)).astype(BF)
    return first, second, third


def travel_rows(z, x, y, nodes):
    node = lax.broadcasted_iota(jnp.int32, (NODE_COLS, LANES), 0)
    node_x = lax.broadcasted_iota(jnp.int32, (NODE_ROWS, LANES), 0).astype(F32)
    scaled = y / SPACING
    cell = jnp.floor(scaled)
    frac = scaled - cell
    cell = cell.astype(jnp.int32)
    x_scaled = x / SPACING
    z_scaled = z / SPACING
    out = []
    for i in range(ROWS):
        hot = jnp.where(node == cell[i : i + 1], 1.0, 0.0).astype(BF)
        hot = jnp.concatenate([hot, hot, hot], axis=0)
        both = jnp.dot(nodes, hot, preferred_element_type=F32)
        count = ND * NODE_ROWS
        along_y = both[:count] + frac[i : i + 1] * both[count:]
        weight_x = jnp.maximum(0.0, 1.0 - jnp.abs(x_scaled[i : i + 1] - node_x))
        z_row = z_scaled[i : i + 1]
        total = None
        for a in range(ND):
            weight_z = jnp.maximum(0.0, 1.0 - jnp.abs(z_row - float(a)))
            term = weight_z * along_y[a * NODE_ROWS : (a + 1) * NODE_ROWS]
            total = term if total is None else total + term
        out.append(jnp.sum(weight_x * total, axis=0, keepdims=True))
    return jnp.concatenate(out, axis=0)


def fill_hats(hats_ref, even, odd, weight_even, weight_odd):
    tiles = HALF // 16
    sample = (
        lax.broadcasted_iota(jnp.int32, (tiles, 16, LANES), 0) * 16
        + lax.broadcasted_iota(jnp.int32, (tiles, 16, LANES), 1)
    ).astype(F32).astype(BF)
    zero = jnp.zeros((), BF)

    def wide(rows, i):
        return jnp.broadcast_to(rows[i : i + 1], (16, LANES)).astype(BF)[None]

    for i in range(ROWS):
        cols = slice(i * LANES, (i + 1) * LANES)
        for half, (index, weight) in enumerate(((even, weight_even), (odd, weight_odd))):
            block = jnp.where(sample == wide(index, i), wide(weight, i), zero)
            hats_ref[half * HALF : (half + 1) * HALF, cols] = block.reshape(HALF, LANES)


def kernel(
    points_ref, nodes_ref, recv_ref, offsets_ref,
    trace_ref, image_ref,
    field, nodes, recv, acc, synth, band, hats, gains, index, weights, picture,
):
    slabs = points_ref.shape[0]
    owners = points_ref.shape[1]
    owned = points_ref.shape[2] // 4
    rows = owned // 2
    chunks = rows // ROWS
    receivers = recv_ref.shape[1]

    for axis in range(2):
        recv[axis] = jnp.broadcast_to(recv_ref[axis], (receivers, LANES))
    synth[...] = jnp.zeros_like(synth)

    def demigrate(slab, _):
        turned = points_ref[slab].T
        for quantity in range(4):
            part = turned[quantity * owned : (quantity + 1) * owned]
            field[quantity] = jnp.concatenate([part[:rows], part[rows:]], axis=1)
        nodes[...] = jnp.concatenate(split3(nodes_ref[slab]), axis=1)
        acc[...] = jnp.zeros_like(acc)

        def step(c, _):
            here = pl.ds(pl.multiple_of(c * ROWS, ROWS), ROWS)
            there = pl.ds(pl.multiple_of(slab * rows + c * ROWS, ROWS), ROWS)
            z, x, y, amplitude = (field[q, here, :] for q in range(4))
            travel = travel_rows(z, x, y, nodes[...])
            first = jnp.floor(travel)
            frac = travel - first
            lower = jnp.floor(first * 0.5)
            is_odd = (first - 2.0 * lower) > 0.5
            even = jnp.where(is_odd, lower + 1.0, lower)
            weight_even = jnp.where(is_odd, frac, 1.0 - frac)
            weight_odd = jnp.where(is_odd, 1.0 - frac, frac)
            index[0, there, :] = even
            index[1, there, :] = lower
            weights[0, there, :] = weight_even
            weights[1, there, :] = weight_odd
            fill_hats(hats, even, lower, amplitude * weight_even, amplitude * weight_odd)
            x_scaled = x * (32.0 / NX)
            y_scaled = y * (32.0 / NX)
            for i in range(ROWS):
                delta_x = recv[0] - x_scaled[i : i + 1]
                delta_y = recv[1] - y_scaled[i : i + 1]
                gain = pl.reciprocal(1.0 + (delta_x * delta_x + delta_y * delta_y), approx=True)
                gains[slab * chunks + c, :, i * LANES : (i + 1) * LANES] = gain.astype(BF)
            acc[...] += lax.dot_general(
                hats[...], gains[slab * chunks + c], (((1,), (1,)), ((), ())),
                preferred_element_type=F32,
            )
            return 0

        lax.fori_loop(0, chunks, step, 0)
        offset = offsets_ref[slab]
        for half in range(2):
            where = pl.ds(offset + half, HALF, stride=2)
            for col in range(0, receivers, LANES):
                part = acc[half * HALF : (half + 1) * HALF, col : col + LANES]
                synth[col // LANES, where, :] += part
        return 0

    lax.fori_loop(0, slabs, demigrate, 0)
    for col in range(0, receivers, LANES):
        trace_ref[col : col + LANES, :] = synth[col // LANES, :SPAN, :].T.astype(BF)

    def migrate(slab, _):
        offset = offsets_ref[slab]
        for half in range(2):
            where = pl.ds(offset + half, HALF, stride=2)
            for col in range(0, receivers, LANES):
                cols = slice(col, col + LANES)
                piece = synth[col // LANES, where, :]
                band[cols, half * HALF : (half + 1) * HALF] = piece.T.astype(BF)

        def step(c, _):
            here = pl.ds(pl.multiple_of(c * ROWS, ROWS), ROWS)
            there = pl.ds(pl.multiple_of(slab * rows + c * ROWS, ROWS), ROWS)
            fill_hats(
                hats, index[0, there, :], index[1, there, :],
                weights[0, there, :], weights[1, there, :],
            )
            product = jnp.dot(band[...], hats[...], preferred_element_type=F32)
            product = product * gains[slab * chunks + c].astype(F32)
            summed = jnp.sum(product, axis=0, keepdims=True)
            picture[here, :] = jnp.concatenate(
                [summed[:, i * LANES : (i + 1) * LANES] for i in range(ROWS)], axis=0
            )
            return 0

        lax.fori_loop(0, chunks, step, 0)
        whole = picture[...] * (1.0 / receivers)
        turned = jnp.concatenate([whole[:, :owners], whole[:, owners:]], axis=0).T
        image_ref[slab, :, :owned] = turned
        image_ref[slab, :, owned:] = jnp.zeros((owners, LANES - owned), F32)
        return 0

    lax.fori_loop(0, slabs, migrate, 0)


def body(
    amplitudes,
    depth_cells,
    lateral_cells,
    jitter,
    tables,
    shot_cells,
    receiver_offsets,
    band_offsets,
):
    owned = amplitudes.shape[1]
    owners = lax.axis_size("shot")
    slabs = lax.axis_size("slab")
    receivers = receiver_offsets.shape[1]
    me = lax.axis_index("slab")

    local = jnp.concatenate(
        [
            depth_cells[0].astype(F32) + jitter[0, 0],
            lateral_cells[0, 0].astype(F32) + jitter[1, 0],
            lateral_cells[1, 0].astype(F32) + jitter[2, 0],
            amplitudes[0],
        ]
    )
    swaps = [[(i, i ^ b) for i in range(slabs)] for b in range(slabs)]

    def swap(array, b):
        return array if b == 0 else lax.ppermute(array, "slab", swaps[b])

    def pick(array, b, axis=0):
        return lax.dynamic_index_in_dim(array, me ^ b, axis, keepdims=False)

    table = jnp.stack([swap(pick(tables[:, 0, :], b), b) for b in range(slabs)])
    table = table.reshape(slabs, ND, NL, NL)
    ahead = jnp.concatenate([table[..., 1:], table[..., -1:]], axis=-1)
    nodes = jnp.stack([table, ahead - table], axis=1)
    nodes = jnp.pad(nodes, ((0, 0), (0, 0), (0, 0), (0, NODE_ROWS - NL), (0, NODE_COLS - NL)))
    nodes = nodes.reshape(slabs, 2 * ND * NODE_ROWS, NODE_COLS)
    offsets = jnp.stack([pick(band_offsets, b) for b in range(slabs)])
    recv = (pick(shot_cells, 0, 1)[:, None] + receiver_offsets).astype(F32) * (32.0 / NX)

    mine = lax.all_to_all(
        jnp.broadcast_to(local[None], (owners, local.shape[0])), "shot", 0, 0
    )
    points = jnp.stack([swap(mine, b) for b in range(slabs)])

    rows = owned // 2
    chunks = rows // ROWS
    vmem = pl.BlockSpec(memory_space=pltpu.VMEM)
    smem = pl.BlockSpec(memory_space=pltpu.SMEM)
    trace, image = pl.pallas_call(
        kernel,
        out_shape=[
            jax.ShapeDtypeStruct((receivers, SPAN), BF),
            jax.ShapeDtypeStruct((slabs, owners, LANES), F32),
        ],
        in_specs=[vmem, vmem, vmem, smem],
        out_specs=[vmem, vmem],
        scratch_shapes=[
            pltpu.VMEM((4, rows, LANES), F32),
            pltpu.VMEM((2 * ND * NODE_ROWS, 3 * NODE_COLS), BF),
            pltpu.VMEM((2, receivers, LANES), F32),
            pltpu.VMEM((BAND, receivers), F32),
            pltpu.VMEM((receivers // LANES, NT, LANES), F32),
            pltpu.VMEM((receivers, BAND), BF),
            pltpu.VMEM((BAND, CHUNK), BF),
            pltpu.VMEM((slabs * chunks, receivers, CHUNK), BF),
            pltpu.VMEM((2, slabs * rows, LANES), F32),
            pltpu.VMEM((2, slabs * rows, LANES), F32),
            pltpu.VMEM((rows, LANES), F32),
        ],
        compiler_params=pltpu.CompilerParams(vmem_limit_bytes=40 * 1024 * 1024),
    )(points, nodes, recv[:, :, None], offsets)

    traces = lax.all_gather(trace, "slab", axis=0)
    synthetic = jnp.pad(traces.astype(F32), ((0, 0), (0, 0), (0, NT - SPAN)))

    part = sum(swap(image[b], b) for b in range(slabs))
    spread = lax.all_to_all(part, "shot", 0, 0)
    return (synthetic, jnp.sum(spread, axis=0)[None, :owned])


def solution(mesh):
    placed = (
        P("slab", "shot"),
        P("slab", "shot"),
        P(None, "slab", "shot"),
        P(None, "slab", "shot"),
        P("shot", "slab", None),
        P(None, "shot"),
        P(),
        P(),
    )
    return jax.shard_map(
        body,
        mesh=mesh,
        in_specs=placed,
        out_specs=(P("shot", None, None), P("slab", "shot")),
        check_vma=False,
    )
```

```python
import functools

import jax
import jax.numpy as jnp
from jax import lax
from jax.experimental import pallas as pl
from jax.experimental.pallas import tpu as pltpu
from jax.sharding import PartitionSpec as P

NX = 512
NT = 1024
BAND = 512
HALF = 256
SPACING = 32
NL = 17
ND = 3
SPAN = 768
LANES = 128
SEGMENTS = 3
ROWS = 8
MXU = 256
PIECE = 16
BF = jnp.bfloat16
F32 = jnp.float32


def travel_octet(z, x, y, table):
    x_scaled = x / SPACING
    z_scaled = z / SPACING
    y_scaled = y / SPACING
    x_cell = jnp.floor(x_scaled)
    y_cell = jnp.floor(y_scaled)
    x_part = x_scaled - x_cell
    y_part = y_scaled - y_cell
    node = (x_cell * NL + y_cell).astype(jnp.int32)
    total = jnp.zeros_like(z)
    corner_weights = ((1.0 - x_part, x_part), (1.0 - y_part, y_part))
    plane_weights = [jnp.maximum(0.0, 1.0 - jnp.abs(z_scaled - float(a))) for a in range(ND)]
    for b in range(2):
        for c in range(2):
            at = node + (b * NL + c)
            lane = at & (LANES - 1)
            block = at >> 7
            first, second = block == 0, block == 1
            value = jnp.zeros_like(z)
            for a in range(ND):
                found = [
                    jnp.take_along_axis(
                        jnp.broadcast_to(table[SEGMENTS * a + k : SEGMENTS * a + k + 1], z.shape),
                        lane, axis=1, mode="promise_in_bounds",
                    )
                    for k in range(SEGMENTS)
                ]
                picked = jnp.where(first, found[0], jnp.where(second, found[1], found[2]))
                value = value + plane_weights[a] * picked
                yield
            total = total + (corner_weights[0][b] * corner_weights[1][c]) * value
    return total


def interleave(*works):
    works = list(works)
    while works:
        for work in list(works):
            if next(work, works) is works:
                works.remove(work)


def kernel(
    points_ref, nodes_ref, recv_ref, offsets_ref,
    trace_ref, image_ref,
    field, recv, synth, band, gains, index, picture,
    near0, near1, *push,
):
    slabs = points_ref.shape[0]
    owners = points_ref.shape[1]
    owned = points_ref.shape[2] // 4
    rows = owned // 2
    steps = rows // ROWS
    receivers = recv_ref.shape[1]
    part = PIECE
    pieces = BAND // part
    near = (near0, near1)

    for k in range(3):
        recv[k] = jnp.broadcast_to(recv_ref[k], (receivers, LANES))
    synth[...] = jnp.zeros_like(synth)
    for slab in range(slabs):
        turned = points_ref[slab].T
        for quantity in range(4):
            piece = turned[quantity * owned : (quantity + 1) * owned]
            field[quantity, slab * rows : (slab + 1) * rows] = jnp.concatenate(
                [piece[:rows], piece[rows:]], axis=1
            )

    def octet(c):
        return pl.ds(pl.multiple_of(c * ROWS, ROWS), ROWS)

    def locate(c, slab, slot):
        z, x, y, amplitude = (field[q, octet(c), :] for q in range(4))
        travel = yield from travel_octet(z, x, y, nodes_ref[slab])
        first = jnp.floor(travel)
        frac = travel - first
        lower = jnp.floor(first * 0.5)
        is_odd = (first - 2.0 * lower) > 0.5
        even = jnp.where(is_odd, lower + 1.0, lower)
        weight_even = jnp.where(is_odd, frac, 1.0 - frac)
        weight_odd = jnp.where(is_odd, 1.0 - frac, frac)
        for k, value in enumerate((even, lower, weight_even, weight_odd)):
            index[k, octet(c), :] = value
        x_near = (x - offsets_ref[slabs]) * (32.0 / NX)
        y_near = (y - offsets_ref[slabs + 1]) * (32.0 / NX)
        square = x_near * x_near + y_near * y_near
        ready = (
            even, lower, amplitude * weight_even, amplitude * weight_odd, x_near, y_near, square
        )
        for k, value in enumerate(ready):
            near[slot][k] = value
        yield

    def radiate(c, pair, slot):
        group = (2 * pair, 2 * pair + 1)
        x_near, y_near, square = (
            [jnp.broadcast_to(near[slot][k, i : i + 1, :], (8, LANES)) for i in group]
            for k in range(4, 7)
        )
        for block in range(0, receivers, 16):
            at = [slice(block + 8 * h, block + 8 * h + 8) for h in range(2)]
            base = [[recv[k, at[h], :] for h in range(2)] for k in range(3)]
            for k, i in enumerate(group):
                gain = jnp.concatenate(
                    [
                        pl.reciprocal(
                            (base[0][h] + square[k])
                            - (base[1][h] * x_near[k] + base[2][h] * y_near[k]),
                            approx=True,
                        )
                        for h in range(2)
                    ],
                    axis=0,
                ).astype(BF)
                gains[c * ROWS + i, block : block + 16, :] = gain
                push[pair][k, block : block + 16, :] = gain
            yield
    def stack(pair, slot, sums):
        group = (2 * pair, 2 * pair + 1)
        pltpu.matmul_push_rhs(
            jnp.concatenate([push[pair][k] for k in range(2)], axis=1),
            pair // 2, pair % 2, transpose=True,
        )
        wide = [
            [jnp.broadcast_to(near[slot][k, i : i + 1, :], (16, LANES)).astype(BF) for i in group]
            for k in range(4)
        ]
        for tile in range(0, HALF, 16):
            sample = (lax.broadcasted_iota(jnp.int32, (16, LANES), 0) + tile).astype(F32).astype(BF)
            for half in range(2):
                hat = [
                    jnp.where(sample == wide[half][k], wide[2 + half][k], jnp.zeros((), BF))
                    for k in range(2)
                ]
                pltpu.matmul_acc_lhs(
                    sums[pair % 2][(half * HALF + tile) // part], jnp.concatenate(hat, axis=1),
                    load_staged_rhs=pair // 2 if tile == 0 and half == 0 else None,
                )
            yield

    def demigrate(*accumulators):
        sums = (accumulators[:pieces], accumulators[pieces:])
        last = slabs * steps - 1

        def phase(c, slot):
            ahead = jnp.minimum(c + 1, last)
            interleave(
                stack(0, slot, sums), stack(1, slot, sums),
                radiate(c, 2, slot), radiate(c, 3, slot),
                locate(ahead, ahead // steps, 1 - slot),
            )
            interleave(
                stack(2, slot, sums), stack(3, slot, sums),
                radiate(ahead, 0, 1 - slot), radiate(ahead, 1, 1 - slot),
            )

        def one_slab(slab, _):
            def two(j, _):
                c = slab * steps + 2 * j
                phase(c, 0)
                phase(c + 1, 1)
                return 0

            lax.fori_loop(0, steps // 2, two, 0)
            offset = offsets_ref[slab]
            for k in range(pieces):
                total = pltpu.matmul_pop(sums[0][k]) + pltpu.matmul_pop(sums[1][k])
                half, start = divmod(k * part, HALF)
                where = pl.ds(offset + half + 2 * start, part, stride=2)
                for col in range(0, receivers, LANES):
                    synth[col // LANES, where, :] += total[:, col : col + LANES]
            return 0

        interleave(locate(0, 0, 0))
        interleave(radiate(0, 0, 0), radiate(0, 1, 0))
        lax.fori_loop(0, slabs, one_slab, 0)

    pl.run_scoped(
        demigrate,
        *[pltpu.ACC(mxu_id=unit)((part, MXU), F32) for unit in range(2) for _ in range(pieces)],
    )

    for col in range(0, receivers, LANES):
        trace_ref[col : col + LANES, :] = synth[col // LANES, :SPAN, :].T.astype(BF)
    for slab in range(slabs):
        offset = offsets_ref[slab]
        for half in range(2):
            where = pl.ds(offset + half, HALF, stride=2)
            for col in range(receivers // LANES):
                band[slab, col, half * HALF : (half + 1) * HALF, :] = synth[col, where, :].astype(BF)

    def migrate(*accumulators):
        groups = [accumulators[g * pieces : (g + 1) * pieces] for g in range(4)]
        sums = (groups[:2], groups[2:])
        sample = lax.broadcasted_iota(jnp.int32, (8, LANES), 0).astype(F32)

        def correlate(c, pair):
            unit, group = pair % 2, pair // 2
            slab = c // steps
            rhs = [gains[c * ROWS + 2 * pair + k] for k in range(2)]
            pltpu.matmul_push_rhs(jnp.concatenate(rhs, axis=1), group, unit)
            yield
            for k in range(pieces):
                lhs = [band[slab, col, k * part : (k + 1) * part, :] for col in range(2)]
                pltpu.matmul_acc_lhs(
                    sums[unit][group][k], jnp.concatenate(lhs, axis=1),
                    load_staged_rhs=group if k == 0 else None,
                )
                yield

        def collect(c, pair):
            unit, group = pair % 2, pair // 2
            found = [[jnp.zeros((8, LANES), F32) for _ in range(2)] for _ in range(2)]
            rows8 = [[index[k, octet(c), :][2 * pair + i : 2 * pair + i + 1] for i in range(2)] for k in range(4)]
            wide = [[jnp.broadcast_to(rows8[k][i], (8, LANES)) for i in range(2)] for k in range(2)]
            for k in range(pieces):
                popped = pltpu.matmul_pop(sums[unit][group][k])
                half, start = divmod(k * part, HALF)
                for block in range(part // 8):
                    here = sample + float(start + block * 8)
                    for i in range(2):
                        value = popped[block * 8 : (block + 1) * 8, i * LANES : (i + 1) * LANES]
                        found[half][i] = jnp.where(here == wide[half][i], value, found[half][i])
                yield
            for i in range(2):
                both = sum(
                    found[half][i] * rows8[2 + half][i].astype(BF).astype(F32) for half in range(2)
                )
                row = 2 * pair + i
                picture[c, row : row + 1, :] = jnp.sum(both, axis=0, keepdims=True)
            yield

        count = slabs * steps

        def step(c, _):
            interleave(correlate(c, 0), correlate(c, 1), collect(c - 1, 2), collect(c - 1, 3))
            interleave(correlate(c, 2), correlate(c, 3), collect(c, 0), collect(c, 1))
            return 0

        interleave(correlate(0, 0), correlate(0, 1))
        interleave(correlate(0, 2), correlate(0, 3), collect(0, 0), collect(0, 1))
        lax.fori_loop(1, count, step, 0)
        interleave(collect(count - 1, 2), collect(count - 1, 3))

    pl.run_scoped(
        migrate,
        *[pltpu.ACC(mxu_id=unit)((part, MXU), F32) for unit in range(2) for _ in range(2 * pieces)],
    )
    for slab in range(slabs):
        whole = picture[slab * steps : (slab + 1) * steps].reshape(rows, LANES) * (1.0 / receivers)
        turned = jnp.concatenate([whole[:, :owners], whole[:, owners:]], axis=0).T
        turned = jnp.concatenate([turned, jnp.zeros((owners, LANES - owned), F32)], axis=1)
        image_ref[pl.ds(offsets_ref[slabs + 2 + slab], owners, stride=slabs), :] = turned


def pack(amplitudes_ref, depth_ref, lateral_ref, jitter_ref, out_ref):
    row = jnp.concatenate(
        [
            depth_ref[...].astype(F32) + jitter_ref[0],
            lateral_ref[0].astype(F32) + jitter_ref[1],
            lateral_ref[1].astype(F32) + jitter_ref[2],
            amplitudes_ref[...],
        ],
        axis=1,
    )
    out_ref[...] = jnp.broadcast_to(row[None], out_ref.shape)


def probe(points, nodes, recv, offsets):
    slabs, owners, width = points.shape
    owned = width // 4
    rows = owned // 2
    receivers = recv.shape[1]
    vmem = pl.BlockSpec(memory_space=pltpu.VMEM)
    smem = pl.BlockSpec(memory_space=pltpu.SMEM)
    return pl.pallas_call(
        kernel,
        out_shape=[
            jax.ShapeDtypeStruct((receivers, SPAN), BF),
            jax.ShapeDtypeStruct((owners * slabs, LANES), F32),
        ],
        in_specs=[vmem, vmem, vmem, smem],
        out_specs=[vmem, vmem],
        scratch_shapes=[
            pltpu.VMEM((4, slabs * rows, LANES), F32),
            pltpu.VMEM((3, receivers, LANES), F32),
            pltpu.VMEM((receivers // LANES, NT, LANES), F32),
            pltpu.VMEM((slabs, receivers // LANES, BAND, LANES), BF),
            pltpu.VMEM((slabs * rows, receivers, LANES), BF),
            pltpu.VMEM((4, slabs * rows, LANES), F32),
            pltpu.VMEM((slabs * rows // ROWS, ROWS, LANES), F32),
            *[pltpu.VMEM((7, ROWS, LANES), F32) for _ in range(2)],
            *[pltpu.VMEM((2, receivers, LANES), BF) for _ in range(ROWS // 2)],
        ],
        compiler_params=pltpu.CompilerParams(vmem_limit_bytes=48 * 1024 * 1024),
    )(points, nodes, recv, offsets)


def body(
    amplitudes,
    depth_cells,
    lateral_cells,
    jitter,
    tables,
    shot_cells,
    receiver_offsets,
    band_offsets,
):
    owned = amplitudes.shape[1]
    owners = lax.axis_size("shot")
    slabs = lax.axis_size("slab")
    receivers = receiver_offsets.shape[1]
    me = lax.axis_index("slab")

    local = pl.pallas_call(
        pack, out_shape=jax.ShapeDtypeStruct((owners, 1, 4 * owned), F32)
    )(amplitudes, depth_cells, lateral_cells, jitter)
    swaps = [[(i, i ^ b) for i in range(slabs)] for b in range(slabs)]

    def swap(array, b):
        return array if b == 0 else lax.ppermute(array, "slab", swaps[b])

    def pick(array, b, axis=0):
        return lax.dynamic_index_in_dim(array, me ^ b, axis, keepdims=False)

    table = jnp.stack([swap(pick(tables[:, 0, :], b), b) for b in range(slabs)])
    nodes = jnp.pad(
        table.reshape(slabs, ND, NL * NL), ((0, 0), (0, 0), (0, SEGMENTS * LANES - NL * NL))
    ).reshape(slabs, ND * SEGMENTS, LANES)
    shot = pick(shot_cells, 0, 1)
    places = me ^ jnp.arange(slabs, dtype=jnp.int32)
    offsets = jnp.concatenate(
        [jnp.stack([pick(band_offsets, b) for b in range(slabs)]), shot, places]
    )
    near = receiver_offsets.astype(F32) * (32.0 / NX)
    recv = jnp.stack([1.0 + near[0] * near[0] + near[1] * near[1], 2.0 * near[0], 2.0 * near[1]])

    mine = lax.all_to_all(local, "shot", 0, 0)[:, 0]
    points = jnp.stack([swap(mine, b) for b in range(slabs)])

    trace, image = probe(points, nodes, recv[:, :, None], offsets)

    spread = lax.all_to_all(image, ("shot", "slab"), 0, 0)

    near_trace = swap(trace, 1)
    far_trace = swap(trace, 2)
    last_trace = swap(far_trace, 1)
    odd, upper = me % 2 == 1, me >= 2

    def ordered(flag, first, second):
        return jnp.where(flag, second, first), jnp.where(flag, first, second)

    low = ordered(odd, trace, near_trace)
    high = ordered(odd, far_trace, last_trace)
    first, third = ordered(upper, low[0], high[0])
    second, fourth = ordered(upper, low[1], high[1])
    synthetic = jnp.pad(
        jnp.stack([first, second, third, fourth]).astype(F32), ((0, 0), (0, 0), (0, NT - SPAN))
    )
    return (synthetic, jnp.sum(spread, axis=0)[None, :owned])


def solution(mesh):
    placed = (
        P("slab", "shot"),
        P("slab", "shot"),
        P(None, "slab", "shot"),
        P(None, "slab", "shot"),
        P("shot", "slab", None),
        P(None, "shot"),
        P(),
        P(),
    )
    return jax.shard_map(
        body,
        mesh=mesh,
        in_specs=placed,
        out_specs=(P("shot", None, None), P("slab", "shot")),
        check_vma=False,
    )
```

```python
import functools

import jax
import jax.numpy as jnp
from jax import lax
from jax.experimental import pallas as pl
from jax.experimental.pallas import tpu as pltpu
from jax.sharding import PartitionSpec as P

NX = 512
NT = 1024
BAND = 512
HALF = 256
SPACING = 32
NL = 17
ND = 3
SPAN = 768
LANES = 128
SEGMENTS = 3
ROWS = 8
MXU = 256
PIECE = 16
VMEM_LIMIT = 8 * 1024 * 1024
BF = jnp.bfloat16
F32 = jnp.float32


def travel_octet(z, x, y, table):
    x_scaled = x / SPACING
    z_scaled = z / SPACING
    y_scaled = y / SPACING
    x_cell = jnp.floor(x_scaled)
    y_cell = jnp.floor(y_scaled)
    x_part = x_scaled - x_cell
    y_part = y_scaled - y_cell
    node = (x_cell * NL + y_cell).astype(jnp.int32)
    total = jnp.zeros_like(z)
    corner_weights = ((1.0 - x_part, x_part), (1.0 - y_part, y_part))
    plane_weights = [jnp.maximum(0.0, 1.0 - jnp.abs(z_scaled - float(a))) for a in range(ND)]
    for b in range(2):
        for c in range(2):
            at = node + (b * NL + c)
            lane = at & (LANES - 1)
            block = at >> 7
            first, second = block == 0, block == 1
            value = jnp.zeros_like(z)
            for a in range(ND):
                found = [
                    jnp.take_along_axis(
                        jnp.broadcast_to(table[SEGMENTS * a + k : SEGMENTS * a + k + 1], z.shape),
                        lane, axis=1, mode="promise_in_bounds",
                    )
                    for k in range(SEGMENTS)
                ]
                picked = jnp.where(first, found[0], jnp.where(second, found[1], found[2]))
                value = value + plane_weights[a] * picked
                yield
            total = total + (corner_weights[0][b] * corner_weights[1][c]) * value
    return total


def interleave(*works):
    works = list(works)
    while works:
        for work in list(works):
            if next(work, works) is works:
                works.remove(work)


def demigrate_kernel(first_slab, total, points_ref, nodes_ref, recv_ref, offsets_ref, *refs):
    previous, refs = (refs[:3], refs[3:]) if first_slab else ((), refs)
    last_call = first_slab + points_ref.shape[0] == total
    (gains, index, synth), refs = refs[:3], refs[3:]
    if last_call:
        trace_ref, refs = refs[0], refs[1:]
    field, recv, near0, near1, *push = refs
    slabs, owners = points_ref.shape[:2]
    owned = points_ref.shape[2] // 4
    rows = owned // 2
    steps = rows // ROWS
    row_base = first_slab * rows
    receivers = recv_ref.shape[1]
    part = PIECE
    pieces = BAND // part
    near = (near0, near1)

    for k in range(3):
        recv[k] = jnp.broadcast_to(recv_ref[k], (receivers, LANES))
    if previous:
        synth[...] = previous[2][...]
    else:
        synth[...] = jnp.zeros_like(synth)
    for slab in range(slabs):
        turned = points_ref[slab].T
        for quantity in range(4):
            piece = turned[quantity * owned : (quantity + 1) * owned]
            field[quantity, slab * rows : (slab + 1) * rows] = jnp.concatenate(
                [piece[:rows], piece[rows:]], axis=1
            )

    def octet(c):
        return pl.ds(pl.multiple_of(c * ROWS, ROWS), ROWS)

    def locate(c, slab, slot):
        z, x, y, amplitude = (field[q, octet(c), :] for q in range(4))
        travel = yield from travel_octet(z, x, y, nodes_ref[slab])
        first = jnp.floor(travel)
        frac = travel - first
        lower = jnp.floor(first * 0.5)
        is_odd = (first - 2.0 * lower) > 0.5
        even = jnp.where(is_odd, lower + 1.0, lower)
        weight_even = jnp.where(is_odd, frac, 1.0 - frac)
        weight_odd = jnp.where(is_odd, 1.0 - frac, frac)
        for k, value in enumerate((even, lower, weight_even, weight_odd)):
            index[k, octet(row_base // ROWS + c), :] = value
        x_near = (x - offsets_ref[total]) * (32.0 / NX)
        y_near = (y - offsets_ref[total + 1]) * (32.0 / NX)
        square = x_near * x_near + y_near * y_near
        ready = (
            even, lower, amplitude * weight_even, amplitude * weight_odd, x_near, y_near, square
        )
        for k, value in enumerate(ready):
            near[slot][k] = value
        yield

    def radiate(c, pair, slot):
        group = (2 * pair, 2 * pair + 1)
        x_near, y_near, square = (
            [jnp.broadcast_to(near[slot][k, i : i + 1, :], (8, LANES)) for i in group]
            for k in range(4, 7)
        )
        for block in range(0, receivers, 16):
            at = [slice(block + 8 * h, block + 8 * h + 8) for h in range(2)]
            base = [[recv[k, at[h], :] for h in range(2)] for k in range(3)]
            for k, i in enumerate(group):
                gain = jnp.concatenate(
                    [
                        pl.reciprocal(
                            (base[0][h] + square[k])
                            - (base[1][h] * x_near[k] + base[2][h] * y_near[k]),
                            approx=True,
                        )
                        for h in range(2)
                    ],
                    axis=0,
                ).astype(BF)
                gains[row_base + c * ROWS + i, block : block + 16, :] = gain
                push[pair][k, block : block + 16, :] = gain
            yield
    def stack(pair, slot, sums):
        group = (2 * pair, 2 * pair + 1)
        pltpu.matmul_push_rhs(
            jnp.concatenate([push[pair][k] for k in range(2)], axis=1),
            pair // 2, pair % 2, transpose=True,
        )
        wide = [
            [jnp.broadcast_to(near[slot][k, i : i + 1, :], (8, LANES)) for i in group]
            for k in range(4)
        ]
        for tile in range(0, HALF, 16):
            sample = lax.broadcasted_iota(jnp.int32, (8, LANES), 0).astype(F32)
            for half in range(2):
                hat = [
                    jnp.concatenate(
                        [
                            jnp.where(sample + float(tile + up) == wide[half][k], wide[2 + half][k], 0.0)
                            for up in (0, 8)
                        ],
                        axis=0,
                    ).astype(BF)
                    for k in range(2)
                ]
                pltpu.matmul_acc_lhs(
                    sums[pair % 2][(half * HALF + tile) // part], jnp.concatenate(hat, axis=1),
                    load_staged_rhs=pair // 2 if tile == 0 and half == 0 else None,
                )
            yield

    def demigrate(*accumulators):
        sums = (accumulators[:pieces], accumulators[pieces:])
        last = slabs * steps - 1

        def phase(c, slot):
            ahead = jnp.minimum(c + 1, last)
            interleave(
                stack(0, slot, sums), stack(1, slot, sums),
                radiate(c, 2, slot), radiate(c, 3, slot),
                locate(ahead, ahead // steps, 1 - slot),
            )
            interleave(
                stack(2, slot, sums), stack(3, slot, sums),
                radiate(ahead, 0, 1 - slot), radiate(ahead, 1, 1 - slot),
            )

        def one_slab(slab, _):
            def two(j, _):
                c = slab * steps + 2 * j
                phase(c, 0)
                phase(c + 1, 1)
                return 0

            lax.fori_loop(0, steps // 2, two, 0)
            offset = offsets_ref[first_slab + slab]
            for k in range(pieces):
                total = pltpu.matmul_pop(sums[0][k]) + pltpu.matmul_pop(sums[1][k])
                half, start = divmod(k * part, HALF)
                where = pl.ds(offset + half + 2 * start, part, stride=2)
                for col in range(0, receivers, LANES):
                    synth[col // LANES, where, :] += total[:, col : col + LANES]
            return 0

        interleave(locate(0, 0, 0))
        interleave(radiate(0, 0, 0), radiate(0, 1, 0))
        lax.fori_loop(0, slabs, one_slab, 0)

    pl.run_scoped(
        demigrate,
        *[pltpu.ACC(mxu_id=unit)((part, MXU), F32) for unit in range(2) for _ in range(pieces)],
    )

    if last_call:
        for col in range(0, receivers, LANES):
            trace_ref[col : col + LANES, :] = synth[col // LANES, :SPAN, :].T.astype(BF)


def migrate_kernel(gains, index, synth, offsets_ref, image_ref, band, picture):
    slabs = band.shape[0]
    receivers = gains.shape[1]
    rows = gains.shape[0] // slabs
    owners = image_ref.shape[0] // slabs
    steps = rows // ROWS
    part = PIECE
    pieces = BAND // part

    def octet(c):
        return pl.ds(pl.multiple_of(c * ROWS, ROWS), ROWS)

    for slab in range(slabs):
        offset = offsets_ref[slab]
        for half in range(2):
            where = pl.ds(offset + half, HALF, stride=2)
            for col in range(receivers // LANES):
                band[slab, col, half * HALF : (half + 1) * HALF, :] = synth[col, where, :].astype(BF)

    def migrate(*accumulators):
        groups = [accumulators[g * pieces : (g + 1) * pieces] for g in range(4)]
        sums = (groups[:2], groups[2:])
        sample = lax.broadcasted_iota(jnp.int32, (8, LANES), 0).astype(F32)

        def correlate(c, pair):
            unit, group = pair % 2, pair // 2
            slab = c // steps
            rhs = [gains[c * ROWS + 2 * pair + k] for k in range(2)]
            pltpu.matmul_push_rhs(jnp.concatenate(rhs, axis=1), group, unit)
            yield
            for k in range(pieces):
                lhs = [band[slab, col, k * part : (k + 1) * part, :] for col in range(2)]
                pltpu.matmul_acc_lhs(
                    sums[unit][group][k], jnp.concatenate(lhs, axis=1),
                    load_staged_rhs=group if k == 0 else None,
                )
                yield

        def collect(c, pair):
            unit, group = pair % 2, pair // 2
            found = [[jnp.zeros((8, LANES), F32) for _ in range(2)] for _ in range(2)]
            rows8 = [[index[k, octet(c), :][2 * pair + i : 2 * pair + i + 1] for i in range(2)] for k in range(4)]
            wide = [[jnp.broadcast_to(rows8[k][i], (8, LANES)) for i in range(2)] for k in range(2)]
            for k in range(pieces):
                popped = pltpu.matmul_pop(sums[unit][group][k])
                half, start = divmod(k * part, HALF)
                for block in range(part // 8):
                    here = sample + float(start + block * 8)
                    for i in range(2):
                        value = popped[block * 8 : (block + 1) * 8, i * LANES : (i + 1) * LANES]
                        found[half][i] = jnp.where(here == wide[half][i], value, found[half][i])
                yield
            for i in range(2):
                both = sum(
                    found[half][i] * rows8[2 + half][i].astype(BF).astype(F32) for half in range(2)
                )
                row = 2 * pair + i
                picture[c, row : row + 1, :] = jnp.sum(both, axis=0, keepdims=True)
            yield

        count = slabs * steps

        def step(c, _):
            interleave(correlate(c, 0), correlate(c, 1), collect(c - 1, 2), collect(c - 1, 3))
            interleave(correlate(c, 2), correlate(c, 3), collect(c, 0), collect(c, 1))
            return 0

        interleave(correlate(0, 0), correlate(0, 1))
        interleave(correlate(0, 2), correlate(0, 3), collect(0, 0), collect(0, 1))
        lax.fori_loop(1, count, step, 0)
        interleave(collect(count - 1, 2), collect(count - 1, 3))

    pl.run_scoped(
        migrate,
        *[pltpu.ACC(mxu_id=unit)((part, MXU), F32) for unit in range(2) for _ in range(2 * pieces)],
    )
    for slab in range(slabs):
        whole = picture[slab * steps : (slab + 1) * steps].reshape(rows, LANES) * (1.0 / receivers)
        turned = jnp.concatenate([whole[:, :owners], whole[:, owners:]], axis=0).T
        blank = jnp.zeros((owners, LANES - turned.shape[1]), F32)
        turned = jnp.concatenate([turned, blank], axis=1)
        image_ref[pl.ds(offsets_ref[slabs + 2 + slab], owners, stride=slabs), :] = turned


def pack(amplitudes_ref, depth_ref, lateral_ref, jitter_ref, out_ref):
    row = jnp.concatenate(
        [
            depth_ref[...].astype(F32) + jitter_ref[0],
            lateral_ref[0].astype(F32) + jitter_ref[1],
            lateral_ref[1].astype(F32) + jitter_ref[2],
            amplitudes_ref[...],
        ],
        axis=1,
    )
    out_ref[...] = jnp.broadcast_to(row[None], out_ref.shape)


def call(kernel, outs, scratch, *args, aliases=None):
    spaces = [pltpu.SMEM if arg.dtype == jnp.int32 else pltpu.VMEM for arg in args]
    return pl.pallas_call(
        kernel,
        out_shape=outs,
        in_specs=[pl.BlockSpec(memory_space=space) for space in spaces],
        out_specs=[pl.BlockSpec(memory_space=pltpu.VMEM) for _ in outs],
        scratch_shapes=scratch,
        input_output_aliases=aliases or {},
        compiler_params=pltpu.CompilerParams(vmem_limit_bytes=VMEM_LIMIT),
    )(*args)


def demigrate_slabs(first_slab, total, points, nodes, recv, offsets, previous):
    slabs, owners, width = points.shape
    rows = width // 8
    receivers = recv.shape[1]
    outs = [
        jax.ShapeDtypeStruct((total * rows, receivers, LANES), BF),
        jax.ShapeDtypeStruct((4, total * rows, LANES), F32),
        jax.ShapeDtypeStruct((receivers // LANES, NT, LANES), F32),
    ]
    if first_slab + slabs == total:
        outs.append(jax.ShapeDtypeStruct((receivers, SPAN), BF))
    return call(
        functools.partial(demigrate_kernel, first_slab, total),
        outs,
        [
            pltpu.VMEM((4, slabs * rows, LANES), F32),
            pltpu.VMEM((3, receivers, LANES), F32),
            *[pltpu.VMEM((7, ROWS, LANES), F32) for _ in range(2)],
            *[pltpu.VMEM((2, receivers, LANES), BF) for _ in range(ROWS // 2)],
        ],
        points, nodes, recv, offsets, *previous,
        aliases={4 + k: k for k in range(len(previous))},
    )


def migrate_slabs(slabs, owners, gains, index, synth, offsets):
    receivers = gains.shape[1]
    rows = gains.shape[0] // slabs
    return call(
        migrate_kernel,
        [jax.ShapeDtypeStruct((owners * slabs, LANES), F32)],
        [
            pltpu.VMEM((slabs, receivers // LANES, BAND, LANES), BF),
            pltpu.VMEM((slabs * rows // ROWS, ROWS, LANES), F32),
        ],
        gains, index, synth, offsets,
    )[0]


def body(
    amplitudes,
    depth_cells,
    lateral_cells,
    jitter,
    tables,
    shot_cells,
    receiver_offsets,
    band_offsets,
):
    owned = amplitudes.shape[1]
    owners = lax.axis_size("shot")
    slabs = lax.axis_size("slab")
    receivers = receiver_offsets.shape[1]
    me = lax.axis_index("slab")

    local = pl.pallas_call(
        pack, out_shape=jax.ShapeDtypeStruct((owners, 1, 4 * owned), F32)
    )(amplitudes, depth_cells, lateral_cells, jitter)
    local, tables = lax.optimization_barrier((local, tables))
    swaps = [[(i, i ^ b) for i in range(slabs)] for b in range(slabs)]

    def swap(array, b):
        return array if b == 0 else lax.ppermute(array, "slab", swaps[b])

    def pick(array, b, axis=0):
        return lax.dynamic_index_in_dim(array, me ^ b, axis, keepdims=False)

    table = jnp.stack([swap(pick(tables[:, 0, :], b), b) for b in range(slabs)])
    nodes = jnp.pad(
        table.reshape(slabs, ND, NL * NL), ((0, 0), (0, 0), (0, SEGMENTS * LANES - NL * NL))
    ).reshape(slabs, ND * SEGMENTS, LANES)
    shot = pick(shot_cells, 0, 1)
    places = me ^ jnp.arange(slabs, dtype=jnp.int32)
    offsets = jnp.concatenate(
        [jnp.stack([pick(band_offsets, b) for b in range(slabs)]), shot, places]
    )
    near = receiver_offsets.astype(F32) * (32.0 / NX)
    recv = jnp.stack([1.0 + near[0] * near[0] + near[1] * near[1], 2.0 * near[0], 2.0 * near[1]])

    mine = lax.all_to_all(local, "shot", 0, 0)[:, 0]
    others = jnp.stack([swap(mine, b) for b in range(1, slabs)])

    recv = recv[:, :, None]
    kept = demigrate_slabs(0, slabs, mine[None], nodes[:1], recv, offsets, [])
    *kept, trace = demigrate_slabs(1, slabs, others, nodes[1:], recv, offsets, kept)
    image = migrate_slabs(slabs, owners, *kept, offsets)

    near_trace = swap(trace, 1)
    far_trace = swap(trace, 2)
    near_trace, far_trace, image = lax.optimization_barrier((near_trace, far_trace, image))
    spread = lax.all_to_all(image, ("shot", "slab"), 0, 0)
    last_trace = swap(far_trace, 1)
    odd, upper = me % 2 == 1, me >= 2

    def ordered(flag, first, second):
        return jnp.where(flag, second, first), jnp.where(flag, first, second)

    low = ordered(odd, trace, near_trace)
    high = ordered(odd, far_trace, last_trace)
    first, third = ordered(upper, low[0], high[0])
    second, fourth = ordered(upper, low[1], high[1])
    synthetic = jnp.pad(
        jnp.stack([first, second, third, fourth]).astype(F32), ((0, 0), (0, 0), (0, NT - SPAN))
    )
    spread, synthetic = lax.optimization_barrier((spread, synthetic))
    return (synthetic, jnp.sum(spread[:, :owned], axis=0)[None])


def solution(mesh):
    placed = (
        P("slab", "shot"),
        P("slab", "shot"),
        P(None, "slab", "shot"),
        P(None, "slab", "shot"),
        P("shot", "slab", None),
        P(None, "shot"),
        P(),
        P(),
    )
    return jax.shard_map(
        body,
        mesh=mesh,
        in_specs=placed,
        out_specs=(P("shot", None, None), P("slab", "shot")),
        check_vma=False,
    )
```

```python
import functools

import jax
import jax.numpy as jnp
from jax import lax
from jax.experimental import pallas as pl
from jax.experimental.pallas import tpu as pltpu
from jax.sharding import PartitionSpec as P

NX = 512
NT = 1024
BAND = 512
HALF = 256
SPACING = 32
NL = 17
ND = 3
SPAN = 768
LANES = 128
ROWS = 8
MXU = 256
PIECE = 16
MIG_SPAN = 6
VMEM_LIMIT = 8 * 1024 * 1024
BF = jnp.bfloat16
F32 = jnp.float32


def travel_octet(z, x, y, table):
    z_scaled = z / SPACING
    parts, cells = [], []
    for scaled in (x / SPACING, y / SPACING):
        cell = jnp.minimum(jnp.floor(scaled), float(NL - 2))
        cells.append(cell)
        parts.append(scaled - cell)
    at = (cells[0] * (NL - 1) + cells[1]).astype(jnp.int32)
    lane = at & (LANES - 1)
    lower = at < LANES
    total = jnp.zeros_like(z)
    sides = [(1.0 - part, part) for part in parts]
    plane_weights = [jnp.maximum(0.0, 1.0 - jnp.abs(z_scaled - float(a))) for a in range(ND)]
    for corner in range(4):
        value = jnp.zeros_like(z)
        for a in range(ND):
            row = 2 * (ND * corner + a)
            found = [
                jnp.take_along_axis(
                    jnp.broadcast_to(table[row + k : row + k + 1], z.shape),
                    lane, axis=1, mode="promise_in_bounds",
                )
                for k in range(2)
            ]
            value = value + plane_weights[a] * jnp.where(lower, found[0], found[1])
            yield
        total = total + (sides[0][corner // 2] * sides[1][corner % 2]) * value
    return total


def interleave(*works):
    works = list(works)
    while works:
        for work in list(works):
            if next(work, works) is works:
                works.remove(work)


def demigrate_kernel(first_slab, total, points_ref, nodes_ref, recv_ref, offsets_ref, *refs):
    previous, refs = (refs[:3], refs[3:]) if first_slab else ((), refs)
    last_call = first_slab + points_ref.shape[0] == total
    (gains, index, synth), refs = refs[:3], refs[3:]
    if last_call:
        trace_ref, refs = refs[0], refs[1:]
    field, recv, near0, near1, *push = refs
    slabs, owners = points_ref.shape[:2]
    owned = points_ref.shape[2] // 4
    rows = owned // 2
    steps = rows // ROWS
    row_base = first_slab * rows
    receivers = recv_ref.shape[1]
    part = PIECE
    pieces = BAND // part
    near = (near0, near1)

    for k in range(3):
        recv[k] = jnp.broadcast_to(recv_ref[k], (receivers, LANES))
    if previous:
        synth[...] = previous[2][...]
    else:
        synth[...] = jnp.zeros_like(synth)
    for slab in range(slabs):
        turned = points_ref[slab].T
        for quantity in range(4):
            piece = turned[quantity * owned : (quantity + 1) * owned]
            field[quantity, slab * rows : (slab + 1) * rows] = jnp.concatenate(
                [piece[:rows], piece[rows:]], axis=1
            )

    def octet(c):
        return pl.ds(pl.multiple_of(c * ROWS, ROWS), ROWS)

    def locate(c, slab, slot):
        z, x, y, amplitude = (field[q, octet(c), :] for q in range(4))
        travel = yield from travel_octet(z, x, y, nodes_ref[slab])
        first = jnp.floor(travel)
        frac = travel - first
        lower = jnp.floor(first * 0.5)
        is_odd = (first - 2.0 * lower) > 0.5
        even = jnp.where(is_odd, lower + 1.0, lower)
        weight_even = jnp.where(is_odd, frac, 1.0 - frac)
        weight_odd = jnp.where(is_odd, 1.0 - frac, frac)
        for k, value in enumerate((even, lower, weight_even, weight_odd)):
            index[k, octet(row_base // ROWS + c), :] = value
        x_near = (x - offsets_ref[total]) * (32.0 / NX)
        y_near = (y - offsets_ref[total + 1]) * (32.0 / NX)
        square = x_near * x_near + y_near * y_near
        ready = (
            even, lower, amplitude * weight_even, amplitude * weight_odd, x_near, y_near, square
        )
        for k, value in enumerate(ready):
            near[slot][k] = value
        yield

    def radiate(c, pair, slot):
        group = (2 * pair, 2 * pair + 1)
        x_near, y_near, square = (
            [jnp.broadcast_to(near[slot][k, i : i + 1, :], (8, LANES)) for i in group]
            for k in range(4, 7)
        )
        for block in range(0, receivers, 16):
            at = [slice(block + 8 * h, block + 8 * h + 8) for h in range(2)]
            base = [[recv[k, at[h], :] for h in range(2)] for k in range(3)]
            for k, i in enumerate(group):
                gain = jnp.concatenate(
                    [
                        pl.reciprocal(
                            (base[0][h] + square[k])
                            - (base[1][h] * x_near[k] + base[2][h] * y_near[k]),
                            approx=True,
                        )
                        for h in range(2)
                    ],
                    axis=0,
                ).astype(BF)
                gains[row_base + c * ROWS + i, block : block + 16, :] = gain
                push[pair][k, block : block + 16, :] = gain
            yield
    def stack(pair, slot, sums):
        group = (2 * pair, 2 * pair + 1)
        pltpu.matmul_push_rhs(
            jnp.concatenate([push[pair][k] for k in range(2)], axis=1),
            pair // 2, pair % 2, transpose=True,
        )
        wide = [
            [jnp.broadcast_to(near[slot][k, i : i + 1, :], (8, LANES)) for i in group]
            for k in range(4)
        ]
        for tile in range(0, HALF, 16):
            sample = lax.broadcasted_iota(jnp.int32, (8, LANES), 0).astype(F32)
            for half in range(2):
                hat = [
                    jnp.concatenate(
                        [
                            jnp.where(sample + float(tile + up) == wide[half][k], wide[2 + half][k], 0.0)
                            for up in (0, 8)
                        ],
                        axis=0,
                    ).astype(BF)
                    for k in range(2)
                ]
                pltpu.matmul_acc_lhs(
                    sums[pair % 2][(half * HALF + tile) // part], jnp.concatenate(hat, axis=1),
                    load_staged_rhs=pair // 2 if tile == 0 and half == 0 else None,
                )
            yield

    def demigrate(*accumulators):
        sums = (accumulators[:pieces], accumulators[pieces:])
        last = slabs * steps - 1

        def phase(c, slot):
            ahead = jnp.minimum(c + 1, last)
            interleave(
                stack(0, slot, sums), stack(1, slot, sums),
                radiate(c, 2, slot), radiate(c, 3, slot),
                locate(ahead, ahead // steps, 1 - slot),
            )
            interleave(
                stack(2, slot, sums), stack(3, slot, sums),
                radiate(ahead, 0, 1 - slot), radiate(ahead, 1, 1 - slot),
            )

        def one_slab(slab, _):
            span = 2 if slabs == 1 else steps

            def several(j, _):
                for k in range(span):
                    phase(slab * steps + j * span + k, k % 2)
                return 0

            lax.fori_loop(0, steps // span, several, 0)
            offset = offsets_ref[first_slab + slab]
            for k in range(pieces):
                total = pltpu.matmul_pop(sums[0][k]) + pltpu.matmul_pop(sums[1][k])
                half, start = divmod(k * part, HALF)
                where = pl.ds(offset + half + 2 * start, part, stride=2)
                for col in range(0, receivers, LANES):
                    synth[col // LANES, where, :] += total[:, col : col + LANES]
            return 0

        interleave(locate(0, 0, 0))
        interleave(radiate(0, 0, 0), radiate(0, 1, 0))
        lax.fori_loop(0, slabs, one_slab, 0)

    pl.run_scoped(
        demigrate,
        *[pltpu.ACC(mxu_id=unit)((part, MXU), F32) for unit in range(2) for _ in range(pieces)],
    )

    if last_call:
        for col in range(0, receivers, LANES):
            trace_ref[col : col + LANES, :] = synth[col // LANES, :SPAN, :].T.astype(BF)


def migrate_kernel(gains, index, synth, offsets_ref, image_ref, band, picture):
    slabs = band.shape[0]
    receivers = gains.shape[1]
    rows = gains.shape[0] // slabs
    owners = image_ref.shape[0] // slabs
    steps = rows // ROWS
    part = PIECE
    pieces = BAND // part

    def octet(c):
        return pl.ds(pl.multiple_of(c * ROWS, ROWS), ROWS)

    for slab in range(slabs):
        offset = offsets_ref[slab]
        for half in range(2):
            where = pl.ds(offset + half, HALF, stride=2)
            for col in range(receivers // LANES):
                band[slab, col, half * HALF : (half + 1) * HALF, :] = synth[col, where, :].astype(BF)

    def migrate(*accumulators):
        groups = [accumulators[g * pieces : (g + 1) * pieces] for g in range(4)]
        sums = (groups[:2], groups[2:])
        sample = lax.broadcasted_iota(jnp.int32, (8, LANES), 0).astype(F32)

        def correlate(c, pair):
            unit, group = pair % 2, pair // 2
            slab = c // steps
            rhs = [gains[c * ROWS + 2 * pair + k] for k in range(2)]
            pltpu.matmul_push_rhs(jnp.concatenate(rhs, axis=1), group, unit)
            yield
            for k in range(pieces):
                lhs = [band[slab, col, k * part : (k + 1) * part, :] for col in range(2)]
                pltpu.matmul_acc_lhs(
                    sums[unit][group][k], jnp.concatenate(lhs, axis=1),
                    load_staged_rhs=group if k == 0 else None,
                )
                yield

        def collect(c, pair):
            unit, group = pair % 2, pair // 2
            found = [[jnp.zeros((8, LANES), F32) for _ in range(2)] for _ in range(2)]
            rows8 = [[index[k, octet(c), :][2 * pair + i : 2 * pair + i + 1] for i in range(2)] for k in range(4)]
            wide = [[jnp.broadcast_to(rows8[k][i], (8, LANES)) for i in range(2)] for k in range(2)]
            for k in range(pieces):
                popped = pltpu.matmul_pop(sums[unit][group][k])
                half, start = divmod(k * part, HALF)
                for block in range(part // 8):
                    here = sample + float(start + block * 8)
                    for i in range(2):
                        value = popped[block * 8 : (block + 1) * 8, i * LANES : (i + 1) * LANES]
                        found[half][i] = jnp.where(here == wide[half][i], value, found[half][i])
                yield
            for i in range(2):
                both = sum(
                    found[half][i] * rows8[2 + half][i].astype(BF).astype(F32) for half in range(2)
                )
                row = 2 * pair + i
                picture[c, row : row + 1, :] = jnp.sum(both, axis=0, keepdims=True)
            yield

        count = slabs * steps

        def octets(j, _):
            for k in range(MIG_SPAN):
                c = MIG_SPAN * j + k
                interleave(correlate(c, 2), correlate(c, 3), collect(c, 0), collect(c, 1))
                ahead = jnp.minimum(c + 1, count - 1)
                interleave(correlate(ahead, 0), correlate(ahead, 1), collect(c, 2), collect(c, 3))
            return 0

        interleave(correlate(0, 0), correlate(0, 1))
        lax.fori_loop(0, count // MIG_SPAN, octets, 0)
        interleave(collect(count - 1, 0), collect(count - 1, 1))

    pl.run_scoped(
        migrate,
        *[pltpu.ACC(mxu_id=unit)((part, MXU), F32) for unit in range(2) for _ in range(2 * pieces)],
    )
    for slab in range(slabs):
        whole = picture[slab * steps : (slab + 1) * steps].reshape(rows, LANES) * (1.0 / receivers)
        turned = jnp.concatenate([whole[:, :owners], whole[:, owners:]], axis=0).T
        blank = jnp.zeros((owners, LANES - turned.shape[1]), F32)
        turned = jnp.concatenate([turned, blank], axis=1)
        image_ref[pl.ds(offsets_ref[slabs + 2 + slab], owners, stride=slabs), :] = turned


def pack(amplitudes_ref, depth_ref, lateral_ref, jitter_ref, out_ref):
    row = jnp.concatenate(
        [
            depth_ref[...].astype(F32) + jitter_ref[0],
            lateral_ref[0].astype(F32) + jitter_ref[1],
            lateral_ref[1].astype(F32) + jitter_ref[2],
            amplitudes_ref[...],
        ],
        axis=1,
    )
    out_ref[...] = jnp.broadcast_to(row[None], out_ref.shape)


def call(kernel, outs, scratch, *args, aliases=None):
    spaces = [pltpu.SMEM if arg.dtype == jnp.int32 else pltpu.VMEM for arg in args]
    return pl.pallas_call(
        kernel,
        out_shape=outs,
        in_specs=[pl.BlockSpec(memory_space=space) for space in spaces],
        out_specs=[pl.BlockSpec(memory_space=pltpu.VMEM) for _ in outs],
        scratch_shapes=scratch,
        input_output_aliases=aliases or {},
        compiler_params=pltpu.CompilerParams(vmem_limit_bytes=VMEM_LIMIT),
    )(*args)


def demigrate_slabs(first_slab, total, points, nodes, recv, offsets, previous):
    slabs, owners, width = points.shape
    rows = width // 8
    receivers = recv.shape[1]
    outs = [
        pltpu.VMEM((total * rows, receivers, LANES), BF),
        pltpu.VMEM((4, total * rows, LANES), F32),
        pltpu.VMEM((receivers // LANES, NT, LANES), F32),
    ]
    if first_slab + slabs == total:
        outs.append(jax.ShapeDtypeStruct((receivers, SPAN), BF))
    return call(
        functools.partial(demigrate_kernel, first_slab, total),
        outs,
        [
            pltpu.VMEM((4, slabs * rows, LANES), F32),
            pltpu.VMEM((3, receivers, LANES), F32),
            *[pltpu.VMEM((7, ROWS, LANES), F32) for _ in range(2)],
            *[pltpu.VMEM((2, receivers, LANES), BF) for _ in range(ROWS // 2)],
        ],
        points, nodes, recv, offsets, *previous,
        aliases={4 + k: k for k in range(len(previous))},
    )


def migrate_slabs(slabs, owners, gains, index, synth, offsets):
    receivers = gains.shape[1]
    rows = gains.shape[0] // slabs
    return call(
        migrate_kernel,
        [jax.ShapeDtypeStruct((owners * slabs, LANES), F32)],
        [
            pltpu.VMEM((slabs, receivers // LANES, BAND, LANES), BF),
            pltpu.VMEM((slabs * rows // ROWS, ROWS, LANES), F32),
        ],
        gains, index, synth, offsets,
    )[0]


def body(
    amplitudes,
    depth_cells,
    lateral_cells,
    jitter,
    tables,
    shot_cells,
    receiver_offsets,
    band_offsets,
):
    owned = amplitudes.shape[1]
    owners = lax.axis_size("shot")
    slabs = lax.axis_size("slab")
    receivers = receiver_offsets.shape[1]
    me = lax.axis_index("slab")

    local = pl.pallas_call(
        pack, out_shape=jax.ShapeDtypeStruct((owners, 1, 4 * owned), F32)
    )(amplitudes, depth_cells, lateral_cells, jitter)
    local, tables = lax.optimization_barrier((local, tables))
    swaps = [[(i, i ^ b) for i in range(slabs)] for b in range(slabs)]

    def swap(array, b):
        return array if b == 0 else lax.ppermute(array, "slab", swaps[b])

    def pick(array, b, axis=0):
        return lax.dynamic_index_in_dim(array, me ^ b, axis, keepdims=False)

    table = jnp.stack([swap(pick(tables[:, 0, :], b), b) for b in range(slabs)])
    table = table.reshape(slabs, ND, NL, NL)
    corners = [
        table[:, :, b : b + NL - 1, c : c + NL - 1].reshape(slabs, 2 * ND, LANES)
        for b in range(2)
        for c in range(2)
    ]
    nodes = jnp.concatenate(corners, axis=1)
    shot = pick(shot_cells, 0, 1)
    places = me ^ jnp.arange(slabs, dtype=jnp.int32)
    offsets = jnp.concatenate(
        [jnp.stack([pick(band_offsets, b) for b in range(slabs)]), shot, places]
    )
    near = receiver_offsets.astype(F32) * (32.0 / NX)
    recv = jnp.stack([1.0 + near[0] * near[0] + near[1] * near[1], 2.0 * near[0], 2.0 * near[1]])

    mine = lax.all_to_all(local, "shot", 0, 0)[:, 0]
    others = jnp.stack([swap(mine, b) for b in range(1, slabs)])

    recv = recv[:, :, None]
    kept = demigrate_slabs(0, slabs, mine[None], nodes[:1], recv, offsets, [])
    *kept, trace = demigrate_slabs(1, slabs, others, nodes[1:], recv, offsets, kept)
    image = migrate_slabs(slabs, owners, *kept, offsets)

    near_trace = swap(trace, 1)
    far_trace = swap(trace, 2)
    spread = lax.all_to_all(image, ("shot", "slab"), 0, 0)
    near_trace, far_trace, _ = lax.optimization_barrier((near_trace, far_trace, image))
    last_trace = swap(far_trace, 1)
    odd, upper = me % 2 == 1, me >= 2

    def ordered(flag, first, second):
        return jnp.where(flag, second, first), jnp.where(flag, first, second)

    low = ordered(odd, trace, near_trace)
    high = ordered(odd, far_trace, last_trace)
    first, third = ordered(upper, low[0], high[0])
    second, fourth = ordered(upper, low[1], high[1])
    synthetic = jnp.pad(
        jnp.stack([first, second, third, fourth]).astype(F32), ((0, 0), (0, 0), (0, NT - SPAN))
    )
    spread, synthetic = lax.optimization_barrier((spread, synthetic))
    return (synthetic, jnp.sum(spread[:, :owned], axis=0)[None])


def solution(mesh):
    placed = (
        P("slab", "shot"),
        P("slab", "shot"),
        P(None, "slab", "shot"),
        P(None, "slab", "shot"),
        P("shot", "slab", None),
        P(None, "shot"),
        P(),
        P(),
    )
    return jax.shard_map(
        body,
        mesh=mesh,
        in_specs=placed,
        out_specs=(P("shot", None, None), P("slab", "shot")),
        check_vma=False,
    )
```

```python
import functools

import jax
import jax.numpy as jnp
from jax import lax
from jax.experimental import pallas as pl
from jax.experimental.pallas import tpu as pltpu
from jax.sharding import PartitionSpec as P

NX = 512
NT = 1024
BAND = 512
HALF = 256
SPACING = 32
NL = 17
ND = 3
SPAN = 768
LANES = 128
ROWS = 8
MXU = 256
PIECE = 16
MIG_SPAN = 6
VMEM_LIMIT = 8 * 1024 * 1024
BF = jnp.bfloat16
F32 = jnp.float32


def travel_octet(z, x, y, table):
    z_scaled = z / SPACING
    parts, cells = [], []
    for scaled in (x / SPACING, y / SPACING):
        cell = jnp.minimum(jnp.floor(scaled), float(NL - 2))
        cells.append(cell)
        parts.append(scaled - cell)
    at = (cells[0] * (NL - 1) + cells[1]).astype(jnp.int32)
    lane = at & (LANES - 1)
    lower = at < LANES
    total = jnp.zeros_like(z)
    sides = [(1.0 - part, part) for part in parts]
    plane_weights = [jnp.maximum(0.0, 1.0 - jnp.abs(z_scaled - float(a))) for a in range(ND)]
    for corner in range(4):
        value = jnp.zeros_like(z)
        for a in range(ND):
            row = 2 * (ND * corner + a)
            found = [
                jnp.take_along_axis(
                    jnp.broadcast_to(table[row + k : row + k + 1], z.shape),
                    lane, axis=1, mode="promise_in_bounds",
                )
                for k in range(2)
            ]
            value = value + plane_weights[a] * jnp.where(lower, found[0], found[1])
            yield
        total = total + (sides[0][corner // 2] * sides[1][corner % 2]) * value
    return total


def interleave(*works):
    works = list(works)
    while works:
        for work in list(works):
            if next(work, works) is works:
                works.remove(work)


def demigrate_kernel(first_slab, total, points_ref, nodes_ref, recv, offsets_ref, *refs):
    previous, refs = (refs[:3], refs[3:]) if first_slab else ((), refs)
    last_call = first_slab + points_ref.shape[0] == total
    (gains, index, synth), refs = refs[:3], refs[3:]
    if last_call:
        trace_ref, refs = refs[0], refs[1:]
    field, near0, near1, *push = refs
    slabs, owners = points_ref.shape[:2]
    owned = points_ref.shape[2] // 4
    rows = owned // 2
    steps = rows // ROWS
    row_base = first_slab * rows
    receivers = recv.shape[1]
    part = PIECE
    pieces = BAND // part
    near = (near0, near1)

    if not previous:
        synth[...] = jnp.zeros_like(synth)
    for slab in range(slabs):
        turned = points_ref[slab].T
        for quantity in range(4):
            piece = turned[quantity * owned : (quantity + 1) * owned]
            field[quantity, slab * rows : (slab + 1) * rows] = jnp.concatenate(
                [piece[:rows], piece[rows:]], axis=1
            )

    def octet(c):
        return pl.ds(pl.multiple_of(c * ROWS, ROWS), ROWS)

    def locate(c, slab, slot):
        z, x, y, amplitude = (field[q, octet(c), :] for q in range(4))
        travel = yield from travel_octet(z, x, y, nodes_ref[slab])
        first = jnp.floor(travel)
        frac = travel - first
        lower = jnp.floor(first * 0.5)
        is_odd = (first - 2.0 * lower) > 0.5
        even = jnp.where(is_odd, lower + 1.0, lower)
        weight_even = jnp.where(is_odd, frac, 1.0 - frac)
        weight_odd = jnp.where(is_odd, 1.0 - frac, frac)
        for k, value in enumerate((even, lower, weight_even, weight_odd)):
            index[k, octet(row_base // ROWS + c), :] = value
        x_near = (x - offsets_ref[total]) * (32.0 / NX)
        y_near = (y - offsets_ref[total + 1]) * (32.0 / NX)
        square = x_near * x_near + y_near * y_near
        ready = (
            even, lower, amplitude * weight_even, amplitude * weight_odd, x_near, y_near, square
        )
        for k, value in enumerate(ready):
            near[slot][k] = value
        yield

    def radiate(c, pair, slot):
        group = (2 * pair, 2 * pair + 1)
        x_near, y_near, square = (
            [jnp.broadcast_to(near[slot][k, i : i + 1, :], (8, LANES)) for i in group]
            for k in range(4, 7)
        )
        for block in range(0, receivers, 16):
            at = [slice(block + 8 * h, block + 8 * h + 8) for h in range(2)]
            base = [[recv[k, at[h], :] for h in range(2)] for k in range(3)]
            for k, i in enumerate(group):
                gain = jnp.concatenate(
                    [
                        pl.reciprocal(
                            (base[0][h] + square[k])
                            - (base[1][h] * x_near[k] + base[2][h] * y_near[k]),
                            approx=True,
                        )
                        for h in range(2)
                    ],
                    axis=0,
                ).astype(BF)
                gains[row_base + c * ROWS + i, block : block + 16, :] = gain
                push[pair][k, block : block + 16, :] = gain
            yield
    def stack(pair, slot, sums):
        group = (2 * pair, 2 * pair + 1)
        pltpu.matmul_push_rhs(
            jnp.concatenate([push[pair][k] for k in range(2)], axis=1),
            pair // 2, pair % 2, transpose=True,
        )
        wide = [
            [jnp.broadcast_to(near[slot][k, i : i + 1, :], (16, LANES)).astype(BF) for i in group]
            for k in range(4)
        ]
        for tile in range(0, HALF, 16):
            sample = (lax.broadcasted_iota(jnp.int32, (16, LANES), 0) + tile).astype(F32).astype(BF)
            for half in range(2):
                hat = [
                    jnp.where(sample == wide[half][k], wide[2 + half][k], jnp.zeros((), BF))
                    for k in range(2)
                ]
                pltpu.matmul_acc_lhs(
                    sums[pair % 2][(half * HALF + tile) // part], jnp.concatenate(hat, axis=1),
                    load_staged_rhs=pair // 2 if tile == 0 and half == 0 else None,
                )
            yield

    def demigrate(*accumulators):
        sums = (accumulators[:pieces], accumulators[pieces:])
        last = slabs * steps - 1

        def phase(c, slot):
            ahead = jnp.minimum(c + 1, last)
            interleave(
                stack(0, slot, sums), stack(1, slot, sums),
                radiate(c, 2, slot), radiate(c, 3, slot),
                locate(ahead, ahead // steps, 1 - slot),
            )
            interleave(
                stack(2, slot, sums), stack(3, slot, sums),
                radiate(ahead, 0, 1 - slot), radiate(ahead, 1, 1 - slot),
            )

        def one_slab(slab, _):
            span = 2 if slabs == 1 else steps

            def several(j, _):
                for k in range(span):
                    phase(slab * steps + j * span + k, k % 2)
                return 0

            lax.fori_loop(0, steps // span, several, 0)
            offset = offsets_ref[first_slab + slab]
            for k in range(pieces):
                total = pltpu.matmul_pop(sums[0][k]) + pltpu.matmul_pop(sums[1][k])
                half, start = divmod(k * part, HALF)
                where = pl.ds(offset + half + 2 * start, part, stride=2)
                for col in range(0, receivers, LANES):
                    synth[col // LANES, where, :] += total[:, col : col + LANES]
            return 0

        interleave(locate(0, 0, 0))
        interleave(radiate(0, 0, 0), radiate(0, 1, 0))
        lax.fori_loop(0, slabs, one_slab, 0)

    pl.run_scoped(
        demigrate,
        *[pltpu.ACC(mxu_id=unit)((part, MXU), F32) for unit in range(2) for _ in range(pieces)],
    )

    if last_call:
        for col in range(0, receivers, LANES):
            trace_ref[col : col + LANES, :] = synth[col // LANES, :SPAN, :].T.astype(BF)


def migrate_kernel(gains, index, synth, offsets_ref, image_ref, band, picture):
    slabs = band.shape[0]
    receivers = gains.shape[1]
    rows = gains.shape[0] // slabs
    owners = image_ref.shape[0] // slabs
    steps = rows // ROWS
    part = PIECE
    pieces = BAND // part

    def octet(c):
        return pl.ds(pl.multiple_of(c * ROWS, ROWS), ROWS)

    for slab in range(slabs):
        offset = offsets_ref[slab]
        for half in range(2):
            where = pl.ds(offset + half, HALF, stride=2)
            for col in range(receivers // LANES):
                band[slab, col, half * HALF : (half + 1) * HALF, :] = synth[col, where, :].astype(BF)

    def migrate(*accumulators):
        groups = [accumulators[g * pieces : (g + 1) * pieces] for g in range(4)]
        sums = (groups[:2], groups[2:])
        sample = lax.broadcasted_iota(jnp.int32, (8, LANES), 0).astype(F32)

        def correlate(c, pair):
            unit, group = pair % 2, pair // 2
            slab = c // steps
            rhs = [gains[c * ROWS + 2 * pair + k] for k in range(2)]
            pltpu.matmul_push_rhs(jnp.concatenate(rhs, axis=1), group, unit)
            yield
            for k in range(pieces):
                lhs = [band[slab, col, k * part : (k + 1) * part, :] for col in range(2)]
                pltpu.matmul_acc_lhs(
                    sums[unit][group][k], jnp.concatenate(lhs, axis=1),
                    load_staged_rhs=group if k == 0 else None,
                )
                yield

        def collect(c, pair):
            unit, group = pair % 2, pair // 2
            found = [[jnp.zeros((8, LANES), F32) for _ in range(2)] for _ in range(2)]
            rows8 = [[index[k, octet(c), :][2 * pair + i : 2 * pair + i + 1] for i in range(2)] for k in range(4)]
            wide = [[jnp.broadcast_to(rows8[k][i], (8, LANES)) for i in range(2)] for k in range(2)]
            for k in range(pieces):
                popped = pltpu.matmul_pop(sums[unit][group][k])
                half, start = divmod(k * part, HALF)
                for block in range(part // 8):
                    here = sample + float(start + block * 8)
                    for i in range(2):
                        value = popped[block * 8 : (block + 1) * 8, i * LANES : (i + 1) * LANES]
                        found[half][i] = jnp.where(here == wide[half][i], value, found[half][i])
                yield
            for i in range(2):
                both = sum(
                    found[half][i] * rows8[2 + half][i].astype(BF).astype(F32) for half in range(2)
                )
                row = 2 * pair + i
                picture[c, row : row + 1, :] = jnp.sum(both, axis=0, keepdims=True)
            yield

        count = slabs * steps

        def octets(j, _):
            for k in range(MIG_SPAN):
                c = MIG_SPAN * j + k
                interleave(correlate(c, 2), correlate(c, 3), collect(c, 0), collect(c, 1))
                ahead = jnp.minimum(c + 1, count - 1)
                interleave(correlate(ahead, 0), correlate(ahead, 1), collect(c, 2), collect(c, 3))
            return 0

        interleave(correlate(0, 0), correlate(0, 1))
        lax.fori_loop(0, count // MIG_SPAN, octets, 0)
        interleave(collect(count - 1, 0), collect(count - 1, 1))

    pl.run_scoped(
        migrate,
        *[pltpu.ACC(mxu_id=unit)((part, MXU), F32) for unit in range(2) for _ in range(2 * pieces)],
    )
    for slab in range(slabs):
        whole = picture[slab * steps : (slab + 1) * steps].reshape(rows, LANES) * (1.0 / receivers)
        turned = jnp.concatenate([whole[:, :owners], whole[:, owners:]], axis=0).T
        blank = jnp.zeros((owners, LANES - turned.shape[1]), F32)
        turned = jnp.concatenate([turned, blank], axis=1)
        image_ref[pl.ds(offsets_ref[slabs + 2 + slab], owners, stride=slabs), :] = turned


def pack(amplitudes_ref, depth_ref, lateral_ref, jitter_ref, out_ref):
    row = jnp.concatenate(
        [
            depth_ref[...].astype(F32) + jitter_ref[0],
            lateral_ref[0].astype(F32) + jitter_ref[1],
            lateral_ref[1].astype(F32) + jitter_ref[2],
            amplitudes_ref[...],
        ],
        axis=1,
    )
    out_ref[...] = jnp.broadcast_to(row[None], out_ref.shape)


def call(kernel, outs, scratch, *args, aliases=None):
    spaces = [pltpu.SMEM if arg.dtype == jnp.int32 else pltpu.VMEM for arg in args]
    return pl.pallas_call(
        kernel,
        out_shape=outs,
        in_specs=[pl.BlockSpec(memory_space=space) for space in spaces],
        out_specs=[pl.BlockSpec(memory_space=pltpu.VMEM) for _ in outs],
        scratch_shapes=scratch,
        input_output_aliases=aliases or {},
        compiler_params=pltpu.CompilerParams(vmem_limit_bytes=VMEM_LIMIT),
    )(*args)


def demigrate_slabs(first_slab, total, points, nodes, recv, offsets, previous):
    slabs, owners, width = points.shape
    rows = width // 8
    receivers = recv.shape[1]
    outs = [
        pltpu.VMEM((total * rows, receivers, LANES), BF),
        pltpu.VMEM((4, total * rows, LANES), F32),
        pltpu.VMEM((receivers // LANES, NT, LANES), F32),
    ]
    if first_slab + slabs == total:
        outs.append(jax.ShapeDtypeStruct((receivers, SPAN), BF))
    return call(
        functools.partial(demigrate_kernel, first_slab, total),
        outs,
        [
            pltpu.VMEM((4, slabs * rows, LANES), F32),
            *[pltpu.VMEM((7, ROWS, LANES), F32) for _ in range(2)],
            *[pltpu.VMEM((2, receivers, LANES), BF) for _ in range(ROWS // 2)],
        ],
        points, nodes, recv, offsets, *previous,
        aliases={4 + k: k for k in range(len(previous))},
    )


def migrate_slabs(slabs, owners, gains, index, synth, offsets):
    receivers = gains.shape[1]
    rows = gains.shape[0] // slabs
    return call(
        migrate_kernel,
        [jax.ShapeDtypeStruct((owners * slabs, LANES), F32)],
        [
            pltpu.VMEM((slabs, receivers // LANES, BAND, LANES), BF),
            pltpu.VMEM((slabs * rows // ROWS, ROWS, LANES), F32),
        ],
        gains, index, synth, offsets,
    )[0]


def body(
    amplitudes,
    depth_cells,
    lateral_cells,
    jitter,
    tables,
    shot_cells,
    receiver_offsets,
    band_offsets,
):
    owned = amplitudes.shape[1]
    owners = lax.axis_size("shot")
    slabs = lax.axis_size("slab")
    receivers = receiver_offsets.shape[1]
    me = lax.axis_index("slab")

    local = pl.pallas_call(
        pack, out_shape=jax.ShapeDtypeStruct((owners, 1, 4 * owned), F32)
    )(amplitudes, depth_cells, lateral_cells, jitter)
    local, tables = lax.optimization_barrier((local, tables))
    swaps = [[(i, i ^ b) for i in range(slabs)] for b in range(slabs)]

    def swap(array, b):
        return array if b == 0 else lax.ppermute(array, "slab", swaps[b])

    def pick(array, b, axis=0):
        return lax.dynamic_index_in_dim(array, me ^ b, axis, keepdims=False)

    table = jnp.stack([swap(pick(tables[:, 0, :], b), b) for b in range(slabs)])
    table = table.reshape(slabs, ND, NL, NL)
    corners = [
        table[:, :, b : b + NL - 1, c : c + NL - 1].reshape(slabs, 2 * ND, LANES)
        for b in range(2)
        for c in range(2)
    ]
    nodes = jnp.concatenate(corners, axis=1)
    shot = pick(shot_cells, 0, 1)
    places = me ^ jnp.arange(slabs, dtype=jnp.int32)
    offsets = jnp.concatenate(
        [jnp.stack([pick(band_offsets, b) for b in range(slabs)]), shot, places]
    )
    near = receiver_offsets.astype(F32) * (32.0 / NX)
    recv = jnp.stack([1.0 + near[0] * near[0] + near[1] * near[1], 2.0 * near[0], 2.0 * near[1]])

    mine = lax.all_to_all(local, "shot", 0, 0)[:, 0]
    others = jnp.stack([swap(mine, b) for b in range(1, slabs)])

    recv = jnp.broadcast_to(recv[:, :, None], (3, receivers, LANES))
    kept = demigrate_slabs(0, slabs, mine[None], nodes[:1], recv, offsets, [])
    *kept, trace = demigrate_slabs(1, slabs, others, nodes[1:], recv, offsets, kept)
    image = migrate_slabs(slabs, owners, *kept, offsets)

    near_trace = swap(trace, 1)
    far_trace = swap(trace, 2)
    spread = lax.all_to_all(image, ("shot", "slab"), 0, 0)
    near_trace, far_trace, _ = lax.optimization_barrier((near_trace, far_trace, image))
    last_trace = swap(far_trace, 1)
    odd, upper = me % 2 == 1, me >= 2

    def ordered(flag, first, second):
        return jnp.where(flag, second, first), jnp.where(flag, first, second)

    low = ordered(odd, trace, near_trace)
    high = ordered(odd, far_trace, last_trace)
    first, third = ordered(upper, low[0], high[0])
    second, fourth = ordered(upper, low[1], high[1])
    synthetic = jnp.pad(
        jnp.stack([first, second, third, fourth]).astype(F32), ((0, 0), (0, 0), (0, NT - SPAN))
    )
    spread, synthetic = lax.optimization_barrier((spread, synthetic))
    return (synthetic, jnp.sum(spread[:, :owned], axis=0)[None])


def solution(mesh):
    placed = (
        P("slab", "shot"),
        P("slab", "shot"),
        P(None, "slab", "shot"),
        P(None, "slab", "shot"),
        P("shot", "slab", None),
        P(None, "shot"),
        P(),
        P(),
    )
    return jax.shard_map(
        body,
        mesh=mesh,
        in_specs=placed,
        out_specs=(P("shot", None, None), P("slab", "shot")),
        check_vma=False,
    )
```

```python
import functools

import jax
import jax.numpy as jnp
from jax import lax
from jax.experimental import pallas as pl
from jax.experimental.pallas import tpu as pltpu
from jax.sharding import PartitionSpec as P

NX = 512
NT = 1024
BAND = 512
HALF = 256
SPACING = 32
NL = 17
ND = 3
SPAN = 768
LANES = 128
ROWS = 8
MXU = 256
PIECE = 16
MIG_SPAN = 12
VMEM_LIMIT = 8 * 1024 * 1024
BF = jnp.bfloat16
F32 = jnp.float32


def travel_octet(z, x, y, table):
    z_scaled = z / SPACING
    parts, cells = [], []
    for scaled in (x / SPACING, y / SPACING):
        cell = jnp.minimum(jnp.floor(scaled), float(NL - 2))
        cells.append(cell)
        parts.append(scaled - cell)
    at = (cells[0] * (NL - 1) + cells[1]).astype(jnp.int32)
    lane = at & (LANES - 1)
    lower = at < LANES
    total = jnp.zeros_like(z)
    sides = [(1.0 - part, part) for part in parts]
    plane_weights = [jnp.maximum(0.0, 1.0 - jnp.abs(z_scaled - float(a))) for a in range(ND)]
    for corner in range(4):
        value = jnp.zeros_like(z)
        for a in range(ND):
            row = 2 * (ND * corner + a)
            found = [
                jnp.take_along_axis(
                    jnp.broadcast_to(table[row + k : row + k + 1], z.shape),
                    lane, axis=1, mode="promise_in_bounds",
                )
                for k in range(2)
            ]
            value = value + plane_weights[a] * jnp.where(lower, found[0], found[1])
            yield
        total = total + (sides[0][corner // 2] * sides[1][corner % 2]) * value
    return total


def interleave(*works):
    works = list(works)
    while works:
        for work in list(works):
            if next(work, works) is works:
                works.remove(work)


def demigrate_kernel(first_slab, total, points_ref, nodes_ref, recv, offsets_ref, *refs):
    previous, refs = (refs[:3], refs[3:]) if first_slab else ((), refs)
    last_call = first_slab + points_ref.shape[0] == total
    (gains, index, synth), refs = refs[:3], refs[3:]
    if last_call:
        trace_ref, refs = refs[0], refs[1:]
    field, near0, near1, *push = refs
    slabs, owners = points_ref.shape[:2]
    owned = points_ref.shape[2] // 4
    rows = owned // 2
    steps = rows // ROWS
    row_base = first_slab * rows
    receivers = recv.shape[1]
    part = PIECE
    pieces = BAND // part
    near = (near0, near1)

    if not previous:
        synth[...] = jnp.zeros_like(synth)
    for slab in range(slabs):
        turned = points_ref[slab].T
        for quantity in range(4):
            piece = turned[quantity * owned : (quantity + 1) * owned]
            field[quantity, slab * rows : (slab + 1) * rows] = jnp.concatenate(
                [piece[:rows], piece[rows:]], axis=1
            )

    def octet(c):
        return pl.ds(pl.multiple_of(c * ROWS, ROWS), ROWS)

    def locate(c, slab, slot):
        z, x, y, amplitude = (field[q, octet(c), :] for q in range(4))
        travel = yield from travel_octet(z, x, y, nodes_ref[slab])
        first = jnp.floor(travel)
        frac = travel - first
        lower = jnp.floor(first * 0.5)
        is_odd = (first - 2.0 * lower) > 0.5
        even = jnp.where(is_odd, lower + 1.0, lower)
        weight_even = jnp.where(is_odd, frac, 1.0 - frac)
        weight_odd = jnp.where(is_odd, 1.0 - frac, frac)
        for k, value in enumerate((even, lower, weight_even, weight_odd)):
            index[k, octet(row_base // ROWS + c), :] = value
        x_near = (x - offsets_ref[total]) * (32.0 / NX)
        y_near = (y - offsets_ref[total + 1]) * (32.0 / NX)
        square = x_near * x_near + y_near * y_near
        ready = (
            even, lower, amplitude * weight_even, amplitude * weight_odd, x_near, y_near, square
        )
        for k, value in enumerate(ready):
            near[slot][k] = value
        yield

    def radiate(c, pair, slot):
        group = (2 * pair, 2 * pair + 1)
        x_near, y_near, square = (
            [jnp.broadcast_to(near[slot][k, i : i + 1, :], (8, LANES)) for i in group]
            for k in range(4, 7)
        )
        for block in range(0, receivers, 16):
            at = [slice(block + 8 * h, block + 8 * h + 8) for h in range(2)]
            base = [[recv[k, at[h], :] for h in range(2)] for k in range(3)]
            for k, i in enumerate(group):
                gain = jnp.concatenate(
                    [
                        pl.reciprocal(
                            (base[0][h] + square[k])
                            - (base[1][h] * x_near[k] + base[2][h] * y_near[k]),
                            approx=True,
                        )
                        for h in range(2)
                    ],
                    axis=0,
                ).astype(BF)
                gains[row_base + c * ROWS + i, block : block + 16, :] = gain
                push[pair][k, block : block + 16, :] = gain
            yield
    def stack(pair, slot, sums):
        group = (2 * pair, 2 * pair + 1)
        pltpu.matmul_push_rhs(
            jnp.concatenate([push[pair][k] for k in range(2)], axis=1),
            pair // 2, pair % 2, transpose=True,
        )
        wide = [
            [jnp.broadcast_to(near[slot][k, i : i + 1, :], (16, LANES)).astype(BF) for i in group]
            for k in range(4)
        ]
        for tile in range(0, HALF, 16):
            sample = (lax.broadcasted_iota(jnp.int32, (16, LANES), 0) + tile).astype(F32).astype(BF)
            for half in range(2):
                hat = [
                    jnp.where(sample == wide[half][k], wide[2 + half][k], jnp.zeros((), BF))
                    for k in range(2)
                ]
                pltpu.matmul_acc_lhs(
                    sums[pair % 2][(half * HALF + tile) // part], jnp.concatenate(hat, axis=1),
                    load_staged_rhs=pair // 2 if tile == 0 and half == 0 else None,
                )
            yield

    def demigrate(*accumulators):
        sums = (accumulators[:pieces], accumulators[pieces:])
        last = slabs * steps - 1

        def phase(c, slot):
            ahead = jnp.minimum(c + 1, last)
            interleave(
                stack(0, slot, sums), stack(1, slot, sums),
                radiate(c, 2, slot), radiate(c, 3, slot),
                locate(ahead, ahead // steps, 1 - slot),
            )
            interleave(
                stack(2, slot, sums), stack(3, slot, sums),
                radiate(ahead, 0, 1 - slot), radiate(ahead, 1, 1 - slot),
            )

        def one_slab(slab, _):
            span = 2 if slabs == 1 else steps

            def several(j, _):
                for k in range(span):
                    phase(slab * steps + j * span + k, k % 2)
                return 0

            lax.fori_loop(0, steps // span, several, 0)
            offset = offsets_ref[first_slab + slab]
            for k in range(pieces):
                total = pltpu.matmul_pop(sums[0][k]) + pltpu.matmul_pop(sums[1][k])
                half, start = divmod(k * part, HALF)
                where = pl.ds(offset + half + 2 * start, part, stride=2)
                for col in range(0, receivers, LANES):
                    synth[col // LANES, where, :] += total[:, col : col + LANES]
            return 0

        interleave(locate(0, 0, 0))
        interleave(radiate(0, 0, 0), radiate(0, 1, 0))
        lax.fori_loop(0, slabs, one_slab, 0)

    pl.run_scoped(
        demigrate,
        *[pltpu.ACC(mxu_id=unit)((part, MXU), F32) for unit in range(2) for _ in range(pieces)],
    )

    if last_call:
        for col in range(0, receivers, LANES):
            trace_ref[col : col + LANES, :] = synth[col // LANES, :SPAN, :].T.astype(BF)


def migrate_kernel(gains, index, synth, offsets_ref, image_ref, band, picture):
    slabs = band.shape[0]
    receivers = gains.shape[1]
    rows = gains.shape[0] // slabs
    owners = image_ref.shape[0] // slabs
    steps = rows // ROWS
    part = PIECE
    pieces = BAND // part

    def octet(c):
        return pl.ds(pl.multiple_of(c * ROWS, ROWS), ROWS)

    for slab in range(slabs):
        offset = offsets_ref[slab]
        for half in range(2):
            where = pl.ds(offset + half, HALF, stride=2)
            for col in range(receivers // LANES):
                band[slab, col, half * HALF : (half + 1) * HALF, :] = synth[col, where, :].astype(BF)

    def migrate(*accumulators):
        groups = [accumulators[g * pieces : (g + 1) * pieces] for g in range(4)]
        sums = (groups[:2], groups[2:])
        sample = lax.broadcasted_iota(jnp.int32, (8, LANES), 0).astype(F32)

        def correlate(c, pair):
            unit, group = pair % 2, pair // 2
            slab = c // steps
            rhs = [gains[c * ROWS + 2 * pair + k] for k in range(2)]
            pltpu.matmul_push_rhs(jnp.concatenate(rhs, axis=1), group, unit)
            yield
            for k in range(pieces):
                lhs = [band[slab, col, k * part : (k + 1) * part, :] for col in range(2)]
                pltpu.matmul_acc_lhs(
                    sums[unit][group][k], jnp.concatenate(lhs, axis=1),
                    load_staged_rhs=group if k == 0 else None,
                )
                yield

        def collect(c, pair):
            unit, group = pair % 2, pair // 2
            found = [[jnp.zeros((8, LANES), F32) for _ in range(2)] for _ in range(2)]
            rows8 = [[index[k, octet(c), :][2 * pair + i : 2 * pair + i + 1] for i in range(2)] for k in range(4)]
            wide = [[jnp.broadcast_to(rows8[k][i], (8, LANES)) for i in range(2)] for k in range(2)]
            for k in range(pieces):
                popped = pltpu.matmul_pop(sums[unit][group][k])
                half, start = divmod(k * part, HALF)
                for block in range(part // 8):
                    here = sample + float(start + block * 8)
                    for i in range(2):
                        value = popped[block * 8 : (block + 1) * 8, i * LANES : (i + 1) * LANES]
                        found[half][i] = jnp.where(here == wide[half][i], value, found[half][i])
                yield
            for i in range(2):
                both = sum(
                    found[half][i] * rows8[2 + half][i].astype(BF).astype(F32) for half in range(2)
                )
                row = 2 * pair + i
                picture[c, row : row + 1, :] = jnp.sum(both, axis=0, keepdims=True)
            yield

        count = slabs * steps

        def octets(j, _):
            for k in range(MIG_SPAN):
                c = MIG_SPAN * j + k
                interleave(correlate(c, 2), correlate(c, 3), collect(c, 0), collect(c, 1))
                ahead = jnp.minimum(c + 1, count - 1)
                interleave(correlate(ahead, 0), correlate(ahead, 1), collect(c, 2), collect(c, 3))
            return 0

        interleave(correlate(0, 0), correlate(0, 1))
        lax.fori_loop(0, count // MIG_SPAN, octets, 0)
        interleave(collect(count - 1, 0), collect(count - 1, 1))

    pl.run_scoped(
        migrate,
        *[pltpu.ACC(mxu_id=unit)((part, MXU), F32) for unit in range(2) for _ in range(2 * pieces)],
    )
    for slab in range(slabs):
        whole = picture[slab * steps : (slab + 1) * steps].reshape(rows, LANES) * (1.0 / receivers)
        turned = jnp.concatenate([whole[:, :owners], whole[:, owners:]], axis=0).T
        blank = jnp.zeros((owners, LANES - turned.shape[1]), F32)
        turned = jnp.concatenate([turned, blank], axis=1)
        image_ref[pl.ds(offsets_ref[slabs + 2 + slab], owners, stride=slabs), :] = turned


def pack(amplitudes_ref, depth_ref, lateral_ref, jitter_ref, out_ref):
    row = jnp.concatenate(
        [
            depth_ref[...].astype(F32) + jitter_ref[0],
            lateral_ref[0].astype(F32) + jitter_ref[1],
            lateral_ref[1].astype(F32) + jitter_ref[2],
            amplitudes_ref[...],
        ],
        axis=1,
    )
    out_ref[...] = jnp.broadcast_to(row[None], out_ref.shape)


def call(kernel, outs, scratch, *args, aliases=None):
    spaces = [pltpu.SMEM if arg.dtype == jnp.int32 else pltpu.VMEM for arg in args]
    return pl.pallas_call(
        kernel,
        out_shape=outs,
        in_specs=[pl.BlockSpec(memory_space=space) for space in spaces],
        out_specs=[pl.BlockSpec(memory_space=pltpu.VMEM) for _ in outs],
        scratch_shapes=scratch,
        input_output_aliases=aliases or {},
        compiler_params=pltpu.CompilerParams(vmem_limit_bytes=VMEM_LIMIT),
    )(*args)


def demigrate_slabs(first_slab, total, points, nodes, recv, offsets, previous):
    slabs, owners, width = points.shape
    rows = width // 8
    receivers = recv.shape[1]
    outs = [
        pltpu.VMEM((total * rows, receivers, LANES), BF),
        pltpu.VMEM((4, total * rows, LANES), F32),
        pltpu.VMEM((receivers // LANES, NT, LANES), F32),
    ]
    if first_slab + slabs == total:
        outs.append(jax.ShapeDtypeStruct((receivers, SPAN), BF))
    return call(
        functools.partial(demigrate_kernel, first_slab, total),
        outs,
        [
            pltpu.VMEM((4, slabs * rows, LANES), F32),
            *[pltpu.VMEM((7, ROWS, LANES), F32) for _ in range(2)],
            *[pltpu.VMEM((2, receivers, LANES), BF) for _ in range(ROWS // 2)],
        ],
        points, nodes, recv, offsets, *previous,
        aliases={4 + k: k for k in range(len(previous))},
    )


def migrate_slabs(slabs, owners, gains, index, synth, offsets):
    receivers = gains.shape[1]
    rows = gains.shape[0] // slabs
    return call(
        migrate_kernel,
        [jax.ShapeDtypeStruct((owners * slabs, LANES), F32)],
        [
            pltpu.VMEM((slabs, receivers // LANES, BAND, LANES), BF),
            pltpu.VMEM((slabs * rows // ROWS, ROWS, LANES), F32),
        ],
        gains, index, synth, offsets,
    )[0]


def body(
    amplitudes,
    depth_cells,
    lateral_cells,
    jitter,
    tables,
    shot_cells,
    receiver_offsets,
    band_offsets,
):
    owned = amplitudes.shape[1]
    owners = lax.axis_size("shot")
    slabs = lax.axis_size("slab")
    receivers = receiver_offsets.shape[1]
    me = lax.axis_index("slab")

    local = pl.pallas_call(
        pack, out_shape=jax.ShapeDtypeStruct((owners, 1, 4 * owned), F32)
    )(amplitudes, depth_cells, lateral_cells, jitter)
    local, tables = lax.optimization_barrier((local, tables))
    swaps = [[(i, i ^ b) for i in range(slabs)] for b in range(slabs)]

    def swap(array, b):
        return array if b == 0 else lax.ppermute(array, "slab", swaps[b])

    def pick(array, b, axis=0):
        return lax.dynamic_index_in_dim(array, me ^ b, axis, keepdims=False)

    table = jnp.stack([swap(pick(tables[:, 0, :], b), b) for b in range(slabs)])
    table = table.reshape(slabs, ND, NL, NL)
    corners = [
        table[:, :, b : b + NL - 1, c : c + NL - 1].reshape(slabs, 2 * ND, LANES)
        for b in range(2)
        for c in range(2)
    ]
    nodes = jnp.concatenate(corners, axis=1)
    shot = pick(shot_cells, 0, 1)
    places = me ^ jnp.arange(slabs, dtype=jnp.int32)
    offsets = jnp.concatenate(
        [jnp.stack([pick(band_offsets, b) for b in range(slabs)]), shot, places]
    )
    near = receiver_offsets.astype(F32) * (32.0 / NX)
    recv = jnp.stack([1.0 + near[0] * near[0] + near[1] * near[1], 2.0 * near[0], 2.0 * near[1]])

    mine = lax.all_to_all(local, "shot", 0, 0)[:, 0]
    others = jnp.stack([swap(mine, b) for b in range(1, slabs)])

    recv = jnp.broadcast_to(recv[:, :, None], (3, receivers, LANES))
    kept = demigrate_slabs(0, slabs, mine[None], nodes[:1], recv, offsets, [])
    *kept, trace = demigrate_slabs(1, slabs, others, nodes[1:], recv, offsets, kept)
    image = migrate_slabs(slabs, owners, *kept, offsets)

    near_trace = swap(trace, 1)
    far_trace = swap(trace, 2)
    spread = lax.all_to_all(image, ("shot", "slab"), 0, 0)
    near_trace, far_trace, _ = lax.optimization_barrier((near_trace, far_trace, image))
    last_trace = swap(far_trace, 1)
    odd, upper = me % 2 == 1, me >= 2

    def ordered(flag, first, second):
        return jnp.where(flag, second, first), jnp.where(flag, first, second)

    low = ordered(odd, trace, near_trace)
    high = ordered(odd, far_trace, last_trace)
    first, third = ordered(upper, low[0], high[0])
    second, fourth = ordered(upper, low[1], high[1])
    synthetic = jnp.pad(
        jnp.stack([first, second, third, fourth]).astype(F32), ((0, 0), (0, 0), (0, NT - SPAN))
    )
    spread, synthetic = lax.optimization_barrier((spread, synthetic))
    return (synthetic, jnp.sum(spread[:, :owned], axis=0)[None])


def solution(mesh):
    placed = (
        P("slab", "shot"),
        P("slab", "shot"),
        P(None, "slab", "shot"),
        P(None, "slab", "shot"),
        P("shot", "slab", None),
        P(None, "shot"),
        P(),
        P(),
    )
    return jax.shard_map(
        body,
        mesh=mesh,
        in_specs=placed,
        out_specs=(P("shot", None, None), P("slab", "shot")),
        check_vma=False,
    )
```
